256 devices in a mesh: row: 32 (over z_lo, y, x), col: 8 (over z_hi, core).
Axes of the slice: x: 4, y: 4, z: 8 (z_hi: 4, z_lo: 2; z = z_hi * 2 + z_lo), core: 2. Of those that a mesh axis runs over, the one named last changes fastest.
Arguments:
- features: bfloat16 [131072, 128], P(('col', 'row')), may hold values from -6 to 6
- weight: bfloat16 [128, 128], replicated, may hold values from -0.5 to 0.5
- cotangent: bfloat16 [131072, 128], P(('row', 'col')), may hold values from -6 to 6
- tile_values: bfloat16 [32, 8, 128, 128, 128], P('row', 'col'), may hold values from -0.09375 to 0.09375
- tile_coords: int32 [32, 8, 128, 2], P('row', 'col'), may hold values from 0 to 127, as said below
- tile_count: int32 [32, 8], P('row', 'col'), may hold values from 64 to 128, as said below
- row_degree: int32 [131072], P(('row', 'col')), may hold values from 1 to 8
- col_degree: int32 [131072], P(('col', 'row')), may hold values from 1 to 8
Outputs:
- layer_out: bfloat16 [131072, 128], P(('row', 'col'))
- grad_input: bfloat16 [131072, 128], P(('col', 'row'))
- grad_weight: float32 [128, 128], replicated
The draws below stay inside these ranges and needn't reach their ends.
Inputs may be any that keep to these rules, and one draw needn't show every extreme that they name: `tile_coords`: entry 0 is a tile row below 32, entry 1 a tile column below 128; padding slots hold coordinates too. A coordinate pair may repeat within a block; such tiles add. `tile_count`: slots at or beyond the count are padding whose values are not part of the matrix. At least half of a block's slots are live, and some block has all 128 live.
All inputs are finite; a program needn't handle non-finite values.
Results may differ from the reference program's by a relative error of at most 0.0054.
Values may be sent and summed in bfloat16 or wider, within the bound.
A program may use at most 64 MiB of HBM per device.

```python
import jax
import jax.numpy as jnp
from jax import lax

F = 128
TB = 128
TILE_DEV = 128
NODES = 131072
ROW_BLOCK = 4096
COL_BLOCK = 16384
ROW_TILES = 32
COL_TILES = 128
N_ROW = 32
N_COL = 8


def draw_tile_coords(key, part):
    key = jax.random.fold_in(key, 11)
    first, second = jax.random.split(key)
    rows = jax.random.randint(first, (N_ROW, N_COL, TILE_DEV, 1), 0, ROW_TILES)
    cols = jax.random.randint(second, (N_ROW, N_COL, TILE_DEV, 1), 0, COL_TILES)
    return jnp.concatenate([rows, cols], axis=3).astype(jnp.int32)


def draw_tile_count(key, part):
    key = jax.random.fold_in(key, 23)
    first, second = jax.random.split(key)
    base = jax.random.randint(first, (N_ROW, N_COL), TILE_DEV // 2, TILE_DEV + 1)
    chosen = jax.random.randint(second, (), 0, N_ROW * N_COL)
    places = jnp.arange(N_ROW * N_COL, dtype=jnp.int32).reshape(N_ROW, N_COL)
    return jnp.where(places == chosen, TILE_DEV, base).astype(jnp.int32)


def touch_ends(drawn, own_key, low, high):
    place = [jax.random.randint(jax.random.fold_in(own_key, axis), (), 0, length) for axis, length in enumerate(drawn.shape)]
    widest = drawn.shape.index(max(drawn.shape))
    beside = place[:widest] + [(place[widest] + 1) % drawn.shape[widest]] + place[widest + 1:]
    return drawn.at[tuple(place)].set(low).at[tuple(beside)].set(high)


def levels(own_key, shape, pieces, least, top_value):
    factor_of = 1.0
    for position, parts in pieces:
        steps = jax.random.uniform(jax.random.fold_in(jax.random.fold_in(own_key, 6), position), (parts,), jnp.float32, least / len(pieces), top_value / len(pieces))
        factor_of = factor_of * jnp.repeat(jnp.exp(steps), shape[position] // parts).reshape((-1,) + (1,) * (len(shape) - 1 - position))
    return factor_of


def scatter_about(rng, dims, scale, reach, pieces=(), kind=jnp.bfloat16):
    values = scale * jax.random.normal(rng, dims, jnp.float32)
    if pieces:
        values = values * levels(rng, dims, pieces, -0.22, 0.18)
    return jnp.clip(values, -reach, reach).astype(kind)


def setup_inputs(seed: int = 0) -> dict:
    arg_keys = jax.random.split(jax.random.key(seed), 9)
    return {
        "features": scatter_about(arg_keys[0], (NODES, F), 1.0, 6.0, ((0, 256),)),
        "weight": scatter_about(arg_keys[1], (F, F), F ** -0.5, 0.5),
        "cotangent": scatter_about(arg_keys[2], (NODES, F), 1.0, 6.0, ((0, 256),)),
        "tile_values": scatter_about(arg_keys[3], (N_ROW, N_COL, TILE_DEV, TB, TB), (max(TB * TILE_DEV * N_COL // ROW_TILES, TB)) ** -0.5, 0.09375, ((0, 32), (1, 8))),
        "tile_coords": draw_tile_coords(jax.random.fold_in(arg_keys[8], 71), 0),
        "tile_count": draw_tile_count(jax.random.fold_in(arg_keys[8], 71), 0),
        "row_degree": touch_ends(jax.random.randint(arg_keys[6], (NODES,), 1, 9), jax.random.fold_in(arg_keys[6], 1), 1, 8).astype(jnp.int32),
        "col_degree": touch_ends(jax.random.randint(arg_keys[7], (NODES,), 1, 9), jax.random.fold_in(arg_keys[7], 1), 1, 8).astype(jnp.int32),
    }


def block_forward(values, coords, count, cols):
    col_tiles = cols.reshape(COL_TILES, TB, F)
    picked = col_tiles[coords[:, 1]]
    prods = jnp.einsum('tij,tjf->tif', values.astype(jnp.float32), picked.astype(jnp.float32))
    live = (jnp.arange(TILE_DEV) < count).astype(jnp.float32)
    table = (coords[:, 0][None, :] == jnp.arange(ROW_TILES)[:, None]).astype(jnp.float32) * live[None, :]
    rows = jnp.einsum('rt,tif->rif', table, prods, precision=lax.Precision.HIGHEST)
    return rows.reshape(ROW_BLOCK, F)

def block_backward(values, coords, count, rows):
    row_tiles = rows.reshape(ROW_TILES, TB, F)
    picked = row_tiles[coords[:, 0]]
    prods = jnp.einsum('tji,tjf->tif', values.astype(jnp.float32), picked.astype(jnp.float32))
    live = (jnp.arange(TILE_DEV) < count).astype(jnp.float32)
    table = (coords[:, 1][None, :] == jnp.arange(COL_TILES)[:, None]).astype(jnp.float32) * live[None, :]
    cols = jnp.einsum('ct,tif->cif', table, prods, precision=lax.Precision.HIGHEST)
    return cols.reshape(COL_BLOCK, F)

def reference(features, weight, cotangent, tile_values, tile_coords, tile_count, row_degree, col_degree):
    row_scale = 1.0 / jnp.sqrt(row_degree.astype(jnp.float32))
    col_scale = 1.0 / jnp.sqrt(col_degree.astype(jnp.float32))
    scaled_in = (features.astype(jnp.float32) * col_scale[:, None]).astype(jnp.bfloat16)

    def forward_row(rindex):

        def step(total, cindex):
            cols = lax.dynamic_slice_in_dim(scaled_in, cindex * COL_BLOCK, COL_BLOCK, 0)
            term = block_forward(tile_values[rindex, cindex], tile_coords[rindex, cindex], tile_count[rindex, cindex], cols)
            return (total + term, None)
        total, _ = lax.scan(step, jnp.zeros((ROW_BLOCK, F), jnp.float32), jnp.arange(N_COL, dtype=jnp.int32))
        return total
    summed = lax.map(forward_row, jnp.arange(N_ROW, dtype=jnp.int32)).reshape(NODES, F)
    hidden = (row_scale[:, None] * summed).astype(jnp.bfloat16)
    layer_out = jnp.dot(hidden, weight, preferred_element_type=jnp.float32).astype(jnp.bfloat16)
    grad_hidden = jnp.dot(cotangent, weight.T, preferred_element_type=jnp.float32)
    scaled_grad = (row_scale[:, None] * grad_hidden).astype(jnp.bfloat16)

    def backward_col(cindex):

        def step(total, rindex):
            rows = lax.dynamic_slice_in_dim(scaled_grad, rindex * ROW_BLOCK, ROW_BLOCK, 0)
            term = block_backward(tile_values[rindex, cindex], tile_coords[rindex, cindex], tile_count[rindex, cindex], rows)
            return (total + term, None)
        total, _ = lax.scan(step, jnp.zeros((COL_BLOCK, F), jnp.float32), jnp.arange(N_ROW, dtype=jnp.int32))
        return total
    back = lax.map(backward_col, jnp.arange(N_COL, dtype=jnp.int32)).reshape(NODES, F)
    grad_input = (col_scale[:, None] * back).astype(jnp.bfloat16)
    grad_weight = jnp.dot(hidden.T, cotangent, preferred_element_type=jnp.float32)
    return (layer_out, grad_input, grad_weight)
```

```python
import jax
import jax.numpy as jnp
from jax import lax
from jax.experimental import pallas as pl
from jax.experimental.pallas import tpu as pltpu
from jax.sharding import PartitionSpec as P

MESH = pl.DeviceIdType.MESH
T = 128
F32 = jnp.float32
BF16 = jnp.bfloat16
ROW_MSGS = 31


def ring(place, step):
    return lax.rem(place + step, 4)


def send(src, dst, ssem, rsem, device):
    pltpu.make_async_remote_copy(
        src_ref=src, dst_ref=dst, send_sem=ssem, recv_sem=rsem, device_id=device, device_id_type=MESH
    ).start()


def sent(src, ssem, rsem, device):
    pltpu.make_async_remote_copy(
        src_ref=src, dst_ref=src, send_sem=ssem, recv_sem=rsem, device_id=device, device_id_type=MESH
    ).wait_send()


def arrived(dst, ssem, rsem, device):
    pltpu.make_async_remote_copy(
        src_ref=dst, dst_ref=dst, send_sem=ssem, recv_sem=rsem, device_id=device, device_id_type=MESH
    ).wait_recv()


def kernel(
    feat, weight, cot, values, coords, count, rdeg, cdeg, out_ref, gin_ref, gw_ref,
    X, V, G, D, R, Q, F, acc, vtab, stab, cscale, rscale,
    b1, b2, b3, c1, e1, x1, x2, x3, xc, e2, bz,
    h1, he, u1, u2, u3, uc,
    w0, a1, a2, a3, a4, s1, s2, full,
    load_sem, tab_sem, row_s, row_r, sum_s, sum_r, col_s, col_r, fsum_s, fsum_r, ar_s, ar_r,
):
    r, c = lax.axis_index("row"), lax.axis_index("col")
    zl, y, x = r // 16, lax.rem(r // 4, 4), lax.rem(r, 4)
    zh, core = c // 2, lax.rem(c, 2)
    z = zh * 2 + zl

    def place(q):
        return x + q * (y - x), y + q * (x - y)

    def row_of(q, zu, p1, p2):
        return zu * 16 + p1 * (1 + 3 * q) + p2 * (4 - 3 * q)

    def unit(ref, q, zu, p1, p2):
        return ref.at[pl.ds(4 * row_of(q, zu, p1, p2) + 2 * q, 2)]

    def on_first(q, step):
        p1, p2 = place(q)
        return (row_of(q, zl, ring(p1, step), p2), c)

    def on_second(q, step):
        p1, p2 = place(q)
        return (row_of(q, zl, p1, ring(p2, step)), c)

    def on_zh(step):
        return (r, ring(zh, step) * 2 + core)

    def on_z(step):
        other = lax.rem(z + step, 8)
        return (lax.rem(other, 2) * 16 + y * 4 + x, (other // 2) * 2 + core)

    partner = ((1 - zl) * 16 + y * 4 + x, c)
    sibling = (r, zh * 2 + 1 - core)
    near, far = zl, 1 - zl
    halves = (0, 1)

    def loop(n, fn):
        def step(i, carry):
            fn(i)
            return carry

        lax.fori_loop(0, n, step, 0)

    def each_half(fn):
        loop(2, fn)

    def each_unit(fn, first=near):
        loop(4, lambda i: fn(lax.rem(i, 2), first + (i // 2) * (1 - 2 * first)))

    load = pltpu.make_async_copy(values, V, load_sem)
    load.start()

    barrier = pltpu.get_barrier_semaphore()
    friends = [sibling]
    friends += [on_first(0, d) for d in (1, 2, 3)]
    friends += [on_first(1, d) for d in (1, 2, 3)]
    friends += [on_z(d) for d in range(1, 8)]
    for friend in friends:
        pl.semaphore_signal(barrier, inc=1, device_id=friend, device_id_type=MESH)

    for k in range(4):
        for deg, scale in ((cdeg, cscale), (rdeg, rscale)):
            line = 1.0 / jnp.sqrt(deg[k : k + 1, :].astype(F32))
            scale[k] = jnp.transpose(jnp.broadcast_to(line, (T, T)))
    for k in range(4):
        rows = pl.ds(k * T, T)
        X[4 * r + k] = (feat[rows, :].astype(F32) * cscale[k]).astype(BF16)
        grad = lax.dot_general(cot[rows, :], weight[...], (((1,), (1,)), ((), ())), preferred_element_type=F32)
        G[4 * c + k] = (rscale[k] * grad).astype(BF16)

    pl.semaphore_wait(barrier, len(friends))

    def row_index1(q, zu, k):
        return q * ROW_MSGS + zu * 3 + k

    def row_index2(q, zu, o, k):
        return q * ROW_MSGS + 6 + (zu * 4 + o) * 3 + k

    def row_indexz(q):
        return q * ROW_MSGS + 30

    def route(zu, k):
        if k == 0:
            return 0, 1
        if k == 1:
            return 0, 3
        return 3 - 2 * zu, 1 + 2 * zu

    def gather1(q, zu, k):
        p1, p2 = place(q)
        back, ahead = route(zu, k)
        piece = unit(X, q, zu, ring(p1, back), p2)
        i = row_index1(q, zu, k)
        send(piece, piece, row_s.at[i], row_r.at[i], on_first(q, ahead))

    def gathered1(q, zu, k):
        p1, p2 = place(q)
        piece = unit(X, q, zu, ring(p1, (3, 1, 2)[k]), p2)
        i = row_index1(q, zu, k)
        arrived(piece, row_s.at[i], row_r.at[i], on_first(q, 1))

    def gather2(q, zu, o, k):
        p1, p2 = place(q)
        back, ahead = route(zu, k)
        piece = unit(X, q, zu, ring(p1, o), ring(p2, back))
        i = row_index2(q, zu, o, k)
        send(piece, piece, row_s.at[i], row_r.at[i], on_second(q, ahead))

    def gathered2(q, zu, o, k):
        p1, p2 = place(q)
        piece = unit(X, q, zu, ring(p1, o), ring(p2, (3, 1, 2)[k]))
        i = row_index2(q, zu, o, k)
        arrived(piece, row_s.at[i], row_r.at[i], on_second(q, 1))

    def shard(ref, zh_of, core_of, first=0, tiles=4):
        return ref.at[pl.ds(4 * (zh_of * 2 + core_of) + first, tiles)]

    def col_piece(owner_step, i, core_of):
        if i in (2, 3, 7, 8):
            return shard(G, ring(zh, owner_step), core_of, 2 * ((i + 1) % 2) if i > 4 else 2 * (i - 2), 2)
        return shard(G, ring(zh, owner_step), core_of)

    def col_send(owner_step, i, device):
        piece = col_piece(owner_step, i, core)
        send(piece, piece, col_s.at[i], col_r.at[i], device)

    def col_arrived(i):
        piece = col_piece((3, 1, 2, 2, 0, 3, 1, 2, 2)[i], i, core if i < 4 else 1 - core)
        arrived(piece, col_s.at[i], col_r.at[i], on_zh(1) if i < 4 else sibling)

    @each_half
    def _(q):
        p1, p2 = place(q)
        piece = unit(X, q, near, p1, p2)
        i = row_indexz(q)
        send(piece, piece, row_s.at[i], row_r.at[i], partner)
        gather1(q, near, 0)
        gather1(q, near, 1)

    col_send(0, 0, on_zh(1))
    col_send(0, 1, on_zh(3))
    col_send(0, 4, sibling)

    @each_half
    def _(q):
        gather2(q, near, 0, 0)
        gather2(q, near, 0, 1)

    own = lax.broadcasted_iota(jnp.int32, (T, T), 0)
    lane = lax.broadcasted_iota(jnp.int32, (T, T), 1)
    live = own < count[0, 0]
    tile_row = jnp.broadcast_to(coords[:, 0:1], (T, T))
    tile_col = jnp.broadcast_to(coords[:, 1:2], (T, T))

    def pick(mask, what):
        return jnp.sum(jnp.where(mask, what, 0), axis=0, keepdims=True)

    for base, major, other in ((0, tile_col, tile_row), (8, tile_row, tile_col)):
        major = jnp.where(live, major, T)
        key = major * T + own
        rank = pick(key < jnp.transpose(key), jnp.ones_like(key))
        rank = jnp.transpose(jnp.broadcast_to(rank, (T, T)))
        here = rank == lane
        target = pick(here, major)
        before = pick(rank + 1 == lane, major + 1) - 1
        vtab[base : base + 1, :] = pick(here, own)
        vtab[base + 1 : base + 2, :] = pick(here, other)
        vtab[base + 2 : base + 3, :] = (target == before).astype(jnp.int32)
        vtab[base + 3 : base + 4, :] = jnp.maximum(pick(major <= lane, jnp.ones_like(key)) - 1, 0)
        vtab[base + 4 : base + 5, :] = jnp.minimum(pick(major == lane, jnp.ones_like(key)), 1)
    table = pltpu.make_async_copy(vtab, stab, tab_sem)
    table.start()

    def products(base, first, last, source, out, contract):
        def step(k, carry):
            tile = V[stab[base, k]]
            rows = source[stab[base + 1, k]]
            prod = lax.dot_general(tile, rows, (((contract,), (0,)), ((), ())), preferred_element_type=F32)
            total = prod + jnp.where(stab[base + 2, k] == 1, acc[...], 0.0)
            acc[...] = total
            out[k] = total.astype(BF16)
            return carry

        lax.fori_loop(first, last, step, 0, unroll=4)

    def spread(base, tiles, segments, out):
        def step(j, carry):
            out[j] = jnp.where(stab[base + 4, j] == 1, segments[stab[base + 3, j]], 0.0).astype(BF16)
            return carry

        lax.fori_loop(0, tiles, step, 0, unroll=4)

    @each_half
    def _(q):
        p1, p2 = place(q)
        i = row_indexz(q)
        arrived(unit(X, q, far, p1, p2), row_s.at[i], row_r.at[i], partner)
        gather1(q, far, 0)
        gather1(q, far, 1)
        gather2(q, far, 0, 0)
        gather2(q, far, 0, 1)

    col_arrived(0)
    col_send(3, 2, on_zh(1))
    col_send(3, 5, sibling)
    col_arrived(1)
    col_send(1, 3, on_zh(3))
    col_send(1, 6, sibling)

    @each_unit
    def _(q, zu):
        gathered1(q, zu, 0)
        gathered1(q, zu, 1)
        gather1(q, zu, 2)
        for o in (3, 1):
            gather2(q, zu, o, 0)
            gather2(q, zu, o, 1)

    col_arrived(2)
    col_send(2, 7, sibling)
    col_arrived(3)
    col_send(2, 8, sibling)

    @each_unit
    def _(q, zu):
        gathered2(q, zu, 0, 0)
        gathered2(q, zu, 0, 1)
        gather2(q, zu, 0, 2)

    @each_unit
    def _(q, zu):
        gathered1(q, zu, 2)
        gather2(q, zu, 2, 0)
        gather2(q, zu, 2, 1)

    for i in range(4, 9):
        col_arrived(i)
    load.wait()
    table.wait()
    acc[...] = jnp.zeros_like(acc)
    products(0, 0, 64, G, R, 0)

    @each_unit
    def _(q, zu):
        for o in (3, 1):
            gathered2(q, zu, o, 0)
            gathered2(q, zu, o, 1)
            gather2(q, zu, o, 2)

    products(0, 64, 128, G, R, 0)

    @each_unit
    def _(q, zu):
        gathered2(q, zu, 2, 0)
        gathered2(q, zu, 2, 1)
        gather2(q, zu, 2, 2)

    spread(0, 128, R, D)

    def sum_index(kind, q, zu, o):
        return ((kind * 2 + q) * 2 + zu) * 4 + o

    def sum_index2(kind, q, zu):
        return 48 + (kind * 2 + q) * 2 + zu

    def ahead_of(zu):
        return 1 + 2 * zu

    def behind_of(zu):
        return 3 - 2 * zu

    def sum_send(kind, q, zu, o):
        p1, p2 = place(q)
        step = behind_of(zu) if kind == 1 else ahead_of(zu)
        if kind == 2:
            src = c1.at[q, zu, o]
        else:
            src = unit(D, q, zu, ring(p1, o), ring(p2, 2 if kind == 0 else step))
        i = sum_index(kind, q, zu, o)
        send(src, (b1, b2, b3)[kind].at[q, zu, o], sum_s.at[i], sum_r.at[i], on_second(q, step))

    def sum_arrived(kind, q, zu, o):
        i = sum_index(kind, q, zu, o)
        arrived((b1, b2, b3)[kind].at[q, zu, o], sum_s.at[i], sum_r.at[i], on_second(q, 1))

    def sum_send2(kind, q, zu):
        step = behind_of(zu) if kind == 1 else ahead_of(zu)
        src = (e1.at[q, zu, 2], e1.at[q, zu, step], xc.at[q, zu])[kind]
        i = sum_index2(kind, q, zu)
        send(src, (x1, x2, x3)[kind].at[q, zu], sum_s.at[i], sum_r.at[i], on_first(q, step))

    def sum_arrived2(kind, q, zu):
        i = sum_index2(kind, q, zu)
        arrived((x1, x2, x3)[kind].at[q, zu], sum_s.at[i], sum_r.at[i], on_first(q, 1))

    def own_unit(q, zu, o, step):
        p1, p2 = place(q)
        return unit(D, q, zu, ring(p1, o), ring(p2, step))[...].astype(F32)

    order = (2, 1, 3, 0)
    for kind in (0, 1):
        for o in order:
            each_unit(lambda q, zu: sum_send(kind, q, zu, o), far)

    @each_unit
    def _(q, zu):
        for o in range(4):
            gathered2(q, zu, o, 2)

    acc[...] = jnp.zeros_like(acc)
    products(8, 0, 128, X, Q, 1)
    spread(8, 32, Q, F)

    def fsum_send(kind, h):
        step = (1 if h == 0 else 3) if kind != 1 else (3 if h == 0 else 1)
        src = (he.at[ring(zh, 2), pl.ds(2 * h, 2)], he.at[ring(zh, step), pl.ds(2 * h, 2)], uc.at[h])[kind]
        i = 4 + 2 * kind + h
        send(src, (u1, u2, u3)[kind].at[h], fsum_s.at[i], fsum_r.at[i], on_zh(step))

    def fsum_arrived(kind, h):
        i = 4 + 2 * kind + h
        arrived((u1, u2, u3)[kind].at[h], fsum_s.at[i], fsum_r.at[i], on_zh(1))

    for d in order:
        owner = ring(zh, d)
        send(shard(F, owner, 1 - core), h1.at[owner], fsum_s.at[d], fsum_r.at[d], sibling)

    for o in order:

        def relay(q, zu):
            sum_arrived(0, q, zu, o)
            c1[q, zu, o] = (b1[q, zu, o].astype(F32) + own_unit(q, zu, o, ahead_of(zu))).astype(BF16)
            sum_send(2, q, zu, o)

        each_unit(relay, far)

    for d in order:
        owner = ring(zh, d)
        arrived(h1.at[owner], fsum_s.at[d], fsum_r.at[d], sibling)
        he[owner] = (h1[owner].astype(F32) + shard(F, owner, core)[...].astype(F32)).astype(BF16)
        if d == 2:
            fsum_send(0, 0)
            fsum_send(0, 1)
    fsum_send(1, 0)
    fsum_send(1, 1)

    def total1(o):
        def add(q, zu):
            sum_arrived(1, q, zu, o)
            sum_arrived(2, q, zu, o)
            e1[q, zu, o] = (
                own_unit(q, zu, o, 0) + b2[q, zu, o].astype(F32) + b3[q, zu, o].astype(F32)
            ).astype(BF16)

        each_unit(add, far)

    total1(2)
    each_unit(lambda q, zu: sum_send2(0, q, zu), far)
    for h in halves:
        fsum_arrived(0, h)
        step = 1 if h == 0 else 3
        uc[h] = (u1[h].astype(F32) + he[ring(zh, step), pl.ds(2 * h, 2)].astype(F32)).astype(BF16)
        fsum_send(2, h)
    total1(1)
    total1(3)
    each_unit(lambda q, zu: sum_send2(1, q, zu), far)

    @each_unit
    def _(q, zu):
        sum_arrived2(0, q, zu)
        xc[q, zu] = (x1[q, zu].astype(F32) + e1[q, zu, ahead_of(zu)].astype(F32)).astype(BF16)
        sum_send2(2, q, zu)

    grad = jnp.zeros((T, T), F32)
    for h in halves:
        fsum_arrived(1, h)
        fsum_arrived(2, h)
        for k in (0, 1):
            n = 2 * h + k
            hidden = he[zh, n].astype(F32) + u2[h, k].astype(F32) + u3[h, k].astype(F32)
            hidden = (rscale[n] * hidden).astype(BF16)
            rows = pl.ds(n * T, T)
            out_ref[rows, :] = jnp.dot(hidden, weight[...], preferred_element_type=F32).astype(BF16)
            grad += lax.dot_general(hidden, cot[rows, :], (((0,), (0,)), ((), ())), preferred_element_type=F32)
    w0[...] = grad

    def ar_send(i, src, dst, device):
        send(src, dst, ar_s.at[i], ar_r.at[i], device)

    def ar_arrived(i, dst, device):
        arrived(dst, ar_s.at[i], ar_r.at[i], device)

    def on_x(d):
        return on_first(0, d)

    def on_y(d):
        return on_first(1, d)

    ar_send(0, w0.at[pl.ds((1 - core) * 64, 64)], a1, sibling)
    total1(0)
    ar_arrived(0, a1, sibling)
    s1[...] = a1[...] + w0[pl.ds(core * 64, 64), :]
    for d in (1, 2, 3):
        ar_send(d, s1.at[pl.ds(ring(x, d) * 16, 16)], a2.at[d - 1], on_x(d))

    def total2(q, zu):
        sum_arrived2(1, q, zu)
        sum_arrived2(2, q, zu)
        return e1[q, zu, 0].astype(F32) + x2[q, zu].astype(F32) + x3[q, zu].astype(F32)

    @each_half
    def _(q):
        e2[q] = total2(q, far).astype(BF16)
        send(e2.at[q], bz.at[q], sum_s.at[60 + q], sum_r.at[60 + q], partner)

    for d in (1, 2, 3):
        ar_arrived(d, a2.at[d - 1], on_x(d))
    a3[y] = s1[pl.ds(x * 16, 16), :] + a2[0] + a2[1] + a2[2]
    for d in (1, 2, 3):
        ar_send(3 + d, a3.at[y], a3.at[y], on_y(d))
    for d in (1, 2, 3):
        ar_arrived(3 + d, a3.at[ring(y, 4 - d)], on_y(d))
    a4[z] = a3[0] + a3[1] + a3[2] + a3[3]
    for d in range(1, 8):
        ar_send(6 + d, a4.at[z], a4.at[z], on_z(d))

    @each_half
    def _(q):
        mine = total2(q, near)
        arrived(bz.at[q], sum_s.at[60 + q], sum_r.at[60 + q], partner)
        mine = mine + bz[q].astype(F32)
        for k in (0, 1):
            n = 2 * q + k
            gin_ref[pl.ds(n * T, T), :] = (cscale[n] * mine[k]).astype(BF16)

    for d in range(1, 8):
        ar_arrived(6 + d, a4.at[lax.rem(z + 8 - d, 8)], on_z(d))
    s2[...] = a4[0] + a4[1] + a4[2] + a4[3] + a4[4] + a4[5] + a4[6] + a4[7]
    mine = pl.ds(core * 64 + x * 16, 16)
    for d in (1, 2, 3):
        ar_send(13 + d, s2, full.at[mine], on_x(d))
    full[mine, :] = s2[...]
    for d in (1, 2, 3):
        ar_arrived(13 + d, full.at[pl.ds(core * 64 + ring(x, 4 - d) * 16, 16)], on_x(d))
    half = full.at[pl.ds(core * 64, 64)]
    ar_send(17, half, half, sibling)
    ar_arrived(17, full.at[pl.ds((1 - core) * 64, 64)], sibling)
    gw_ref[...] = full[...]

    loop(62, lambda i: sent(X.at[pl.ds(0, 2)], row_s.at[i], row_r.at[i], sibling))
    loop(62, lambda i: sent(D.at[pl.ds(0, 2)], sum_s.at[i], sum_r.at[i], sibling))
    for i in range(9):
        sent(G.at[pl.ds(0, 2 if i in (2, 3, 7, 8) else 4)], col_s.at[i], col_r.at[i], sibling)
    for i in range(10):
        sent(F.at[pl.ds(0, 4 if i < 4 else 2)], fsum_s.at[i], fsum_r.at[i], sibling)
    for i in range(18):
        sent(full.at[pl.ds(0, 64 if i in (0, 17) else 16)], ar_s.at[i], ar_r.at[i], sibling)


def body(features, weight, cotangent, tile_values, tile_coords, tile_count, row_degree, col_degree):
    vmem = pl.BlockSpec(memory_space=pltpu.VMEM)
    units = lambda *lead: pltpu.VMEM((*lead, 2, T, T), BF16)
    sems = lambda n: pltpu.SemaphoreType.DMA((n,))
    rows = lambda n: pltpu.VMEM((n, T), F32)
    return pl.pallas_call(
        kernel,
        out_shape=(
            jax.ShapeDtypeStruct((512, T), BF16),
            jax.ShapeDtypeStruct((512, T), BF16),
            jax.ShapeDtypeStruct((T, T), F32),
        ),
        in_specs=[
            vmem, vmem, vmem, pl.BlockSpec(memory_space=pl.ANY), vmem,
            pl.BlockSpec(memory_space=pltpu.SMEM), vmem, vmem,
        ],
        out_specs=(vmem, vmem, vmem),
        scratch_shapes=[
            pltpu.VMEM((128, T, T), BF16),
            pltpu.VMEM((128, T, T), BF16),
            pltpu.VMEM((32, T, T), BF16),
            pltpu.VMEM((128, T, T), BF16),
            pltpu.VMEM((128, T, T), BF16),
            pltpu.VMEM((128, T, T), BF16),
            pltpu.VMEM((32, T, T), BF16),
            rows(T),
            pltpu.VMEM((16, T), jnp.int32),
            pltpu.SMEM((16, T), jnp.int32),
            pltpu.VMEM((4, T, T), F32),
            pltpu.VMEM((4, T, T), F32),
            units(2, 2, 4), units(2, 2, 4), units(2, 2, 4), units(2, 2, 4), units(2, 2, 4),
            units(2, 2), units(2, 2), units(2, 2), units(2, 2), units(2), units(2),
            pltpu.VMEM((4, 4, T, T), BF16),
            pltpu.VMEM((4, 4, T, T), BF16),
            units(2), units(2), units(2), units(2),
            rows(T),
            rows(64),
            pltpu.VMEM((3, 16, T), F32),
            pltpu.VMEM((4, 16, T), F32),
            pltpu.VMEM((8, 16, T), F32),
            rows(64),
            rows(16),
            rows(T),
            pltpu.SemaphoreType.DMA, pltpu.SemaphoreType.DMA,
            sems(62), sems(62), sems(62), sems(62), sems(9), sems(9), sems(10), sems(10), sems(18), sems(18),
        ],
        compiler_params=pltpu.CompilerParams(
            collective_id=0, has_side_effects=True, vmem_limit_bytes=56 * 1024 * 1024
        ),
    )(
        features,
        weight,
        cotangent,
        tile_values[0, 0],
        tile_coords[0, 0],
        tile_count,
        row_degree.reshape(4, T),
        col_degree.reshape(4, T),
    )


def solution(mesh):
    in_specs = (
        P(("col", "row"), None),
        P(),
        P(("row", "col"), None),
        P("row", "col", None, None, None),
        P("row", "col", None, None),
        P("row", "col"),
        P(("row", "col")),
        P(("col", "row")),
    )
    out_specs = (P(("row", "col"), None), P(("col", "row"), None), P())
    return jax.shard_map(body, mesh=mesh, in_specs=in_specs, out_specs=out_specs, check_vma=False)
```

```python
import jax
import jax.numpy as jnp
from jax import lax
from jax.experimental import pallas as pl
from jax.experimental.pallas import tpu as pltpu
from jax.sharding import PartitionSpec as P

MESH = pl.DeviceIdType.MESH
T = 128
F32 = jnp.float32
BF16 = jnp.bfloat16


def ring(place, step):
    return lax.rem(place + step, 4)


def send(src, dst, ssem, rsem, device):
    pltpu.make_async_remote_copy(
        src_ref=src, dst_ref=dst, send_sem=ssem, recv_sem=rsem, device_id=device, device_id_type=MESH
    ).start()


def sent(src, ssem, rsem, device):
    pltpu.make_async_remote_copy(
        src_ref=src, dst_ref=src, send_sem=ssem, recv_sem=rsem, device_id=device, device_id_type=MESH
    ).wait_send()


def arrived(dst, ssem, rsem, device):
    pltpu.make_async_remote_copy(
        src_ref=dst, dst_ref=dst, send_sem=ssem, recv_sem=rsem, device_id=device, device_id_type=MESH
    ).wait_recv()


def kernel(
    feat, weight, cot, values, coords, count, rdeg, cdeg, out_ref, gin_ref, gw_ref,
    X, V, C, G, D, R, Q, F, acc, vtab, stab, cscale, rscale, fe, we, co, rd, cd, lo, gi,
    b1, b2, b3, c1, e1, x1, x2, x3, xc, e2, bz,
    h1, he, u1, u2, u3, uc,
    w0, a1, a2, a3, a4, s1, full, pad,
    load_sem, in_sem, out_sem, tab_sem, send_sem, row_r, sum_r, col_r, fsum_r, ar_r,
):
    r, c = lax.axis_index("row"), lax.axis_index("col")
    zl, y, x = r // 16, lax.rem(r // 4, 4), lax.rem(r, 4)
    zh, core = c // 2, lax.rem(c, 2)
    z = zh * 2 + zl

    px, py = [ring(x, d) for d in range(4)], [ring(y, d) for d in range(4)]
    on_x = [(zl * 16 + y * 4 + px[d], c) for d in range(4)]
    on_y = [(zl * 16 + py[d] * 4 + x, c) for d in range(4)]
    places = ((px, py), (py, px))
    devices = ((on_x, on_y), (on_y, on_x))

    def along(items, step):
        if isinstance(step, int):
            return items[step]
        return jnp.where(step == 1, items[1], items[3])

    def device(q, axis, step):
        there = devices[q][axis]
        if isinstance(step, int):
            return there[step]
        return (jnp.where(step == 1, there[1][0], there[3][0]), c)

    def unit(ref, q, zu, p1, p2):
        i, j = (p1, p2) if q == 0 else (p2, p1)
        return ref.at[pl.ds(64 * zu + 16 * j + 4 * i + 2 * q, 2)]

    def on_zh(step):
        return (r, ring(zh, step) * 2 + core)

    def on_z(step):
        other = lax.rem(z + step, 8)
        return (lax.rem(other, 2) * 16 + y * 4 + x, (other // 2) * 2 + core)

    partner = ((1 - zl) * 16 + y * 4 + x, c)
    sibling = (r, zh * 2 + 1 - core)
    near, far = zl, 1 - zl
    halves = (0, 1)

    ins = [
        pltpu.make_async_copy(src, dst, in_sem.at[i])
        for i, (src, dst) in enumerate(
            ((cdeg, cd), (feat, fe), (rdeg, rd), (cot, C.at[c, pl.ds(0, 512)]), (weight, we), (coords, co))
        )
    ]
    for copy in ins:
        copy.start()
    load = pltpu.make_async_copy(values, V, load_sem)
    load.start()

    barrier = pltpu.get_barrier_semaphore()
    friends = [sibling]
    friends += [on_x[d] for d in (1, 2, 3)]
    friends += [on_y[d] for d in (1, 2, 3)]
    friends += [on_z(d) for d in range(1, 8)]
    for friend in friends:
        pl.semaphore_signal(barrier, inc=1, device_id=friend, device_id_type=MESH)

    def column(line):
        return jnp.transpose(jnp.broadcast_to(1.0 / jnp.sqrt(line.astype(F32)), (T, T)))

    for copy in ins:
        copy.wait()
    for k in range(4):
        cscale[k] = column(cd[k : k + 1, :])
        X[4 * r + k] = (fe[pl.ds(k * T, T), :].astype(F32) * cscale[k]).astype(BF16)
    line = lax.broadcasted_iota(jnp.int32, (16, T), 0)
    tail = jnp.ones((16, T), F32)
    for k in range(4):
        tail = jnp.where(line == k, jnp.broadcast_to(rd[k : k + 1, :].astype(F32), (16, T)), tail)
    C[c, pl.ds(512, 16), :] = tail.astype(BF16)

    pl.semaphore_wait(barrier, len(friends))

    def route(zu, k):
        if k == 0:
            return 0, 1
        if k == 1:
            return 0, 3
        return 3 - 2 * zu, 1 + 2 * zu

    def gather1(q, zu, k):
        first, second = places[q]
        back, ahead = route(zu, k)
        piece = unit(X, q, zu, along(first, back), second[0])
        send(piece, piece, send_sem.at[0], row_r.at[6 * zu + k // 2], device(q, 0, ahead))

    def gather2(q, zu, o, k):
        first, second = places[q]
        back, ahead = route(zu, k)
        piece = unit(X, q, zu, first[o], along(second, back))
        i = 13 if k == 2 else 6 * zu + 2 + o
        send(piece, piece, send_sem.at[0], row_r.at[i], device(q, 1, ahead))

    def gathered(i, tiles):
        arrived(X.at[pl.ds(0, tiles)], send_sem.at[0], row_r.at[i], sibling)

    def shard(ref, zh_of, core_of):
        return ref.at[pl.ds(4 * (zh_of * 2 + core_of), 4)]

    def col_piece(owner_step, i, core_of):
        whose = ring(zh, owner_step) * 2 + core_of
        if i in (2, 7):
            return C.at[whose, pl.ds(0, 256)]
        if i in (3, 8):
            return C.at[whose, pl.ds(256, 272)]
        return C.at[whose]

    def col_send(owner_step, i, device):
        piece = col_piece(owner_step, i, core)
        send(piece, piece, send_sem.at[1], col_r.at[(0, 0, 1, 1, 2, 3, 3, 4, 4)[i]], device)

    def col_arrived(i):
        n = (2, 1, 1, 2, 1)[i]
        arrived(C.at[pl.ds(0, n)], send_sem.at[1], col_r.at[i], sibling)

    def scaled_grad(owner):
        lines = C[owner, pl.ds(512, 16), :].astype(F32)
        for k in range(4):
            n = 4 * owner + k
            scale = column(lines[k : k + 1, :])
            rscale[n] = scale
            grad = lax.dot_general(
                C[owner, pl.ds(k * T, T), :], we[...], (((1,), (1,)), ((), ())), preferred_element_type=F32
            )
            G[n] = (scale * grad).astype(BF16)

    for q in halves:
        piece = unit(X, q, near, places[q][0][0], places[q][1][0])
        send(piece, piece, send_sem.at[0], row_r.at[12], partner)
    for q in halves:
        gather1(q, near, 0)
        gather1(q, near, 1)
    for q in halves:
        gather2(q, near, 0, 0)
        gather2(q, near, 0, 1)
    col_send(0, 0, on_zh(1))
    col_send(0, 1, on_zh(3))
    col_send(0, 4, sibling)

    own = lax.broadcasted_iota(jnp.int32, (T, T), 0)
    lane = lax.broadcasted_iota(jnp.int32, (T, T), 1)
    live = own < count[0, 0]
    by_row = jnp.transpose(jnp.broadcast_to(co[0:1, :], (T, T)))
    by_col = jnp.transpose(jnp.broadcast_to(co[1:2, :], (T, T)))
    def pick(mask, what):
        return jnp.sum(jnp.where(mask, what, 0), axis=0, keepdims=True)

    for base, major, other in ((0, by_col, by_row), (8, by_row, by_col)):
        major = jnp.where(live, major, T)
        key = major * T + own
        rank = pick(key < jnp.transpose(key), jnp.ones_like(key))
        rank = jnp.transpose(jnp.broadcast_to(rank, (T, T)))
        here = rank == lane
        target = pick(here, major)
        before = pick(rank + 1 == lane, major + 1) - 1
        vtab[base : base + 1, :] = pick(here, own)
        vtab[base + 1 : base + 2, :] = pick(here, other)
        vtab[base + 2 : base + 3, :] = (target == before).astype(jnp.int32)
        vtab[base + 3 : base + 4, :] = jnp.maximum(pick(major <= lane, jnp.ones_like(key)) - 1, 0)
        vtab[base + 4 : base + 5, :] = jnp.minimum(pick(major == lane, jnp.ones_like(key)), 1)
    table = pltpu.make_async_copy(vtab, stab, tab_sem)
    table.start()

    def products(base, first, last, source, out, contract):
        def step(k, carry):
            tile = V[stab[base, k]]
            rows = source[stab[base + 1, k]]
            prod = lax.dot_general(tile, rows, (((contract,), (0,)), ((), ())), preferred_element_type=F32)
            total = prod + jnp.where(stab[base + 2, k] == 1, acc[...], 0.0)
            acc[...] = total
            out[k] = total.astype(out.dtype)
            return carry

        lax.fori_loop(first, last, step, 0, unroll=4)

    def segment(base, segments, j):
        return jnp.where(stab[base + 4, j] == 1, segments[stab[base + 3, j]], 0.0)

    def spread(first, last):
        def step(j, carry):
            D[j] = segment(0, R, j).astype(BF16)
            return carry

        lax.fori_loop(first, last, step, 0, unroll=4)

    def turn1(zu):
        gathered(6 * zu, 8)
        for q in halves:
            gather1(q, zu, 2)
        for o in (3, 1):
            for q in halves:
                gather2(q, zu, o, 0)
                gather2(q, zu, o, 1)

    def turn2(zu):
        gathered(6 * zu + 1, 4)
        for q in halves:
            gather2(q, zu, 2, 0)
            gather2(q, zu, 2, 1)

    def turn3(zu, o):
        gathered(6 * zu + 2 + o, 8)
        for q in halves:
            gather2(q, zu, o, 2)

    turn1(near)
    gathered(12, 4)
    for q in halves:
        gather1(q, far, 0)
        gather1(q, far, 1)
    for q in halves:
        gather2(q, far, 0, 0)
        gather2(q, far, 0, 1)
    turn2(near)
    turn1(far)
    turn3(near, 0)
    scaled_grad(c)
    col_arrived(2)
    scaled_grad(zh * 2 + 1 - core)
    turn2(far)
    turn3(near, 3)
    turn3(near, 1)
    col_arrived(0)
    col_send(3, 2, on_zh(1))
    col_send(1, 3, on_zh(3))
    col_send(3, 5, sibling)
    col_send(1, 6, sibling)
    turn3(far, 0)
    scaled_grad(ring(zh, 3) * 2 + core)
    scaled_grad(ring(zh, 1) * 2 + core)
    turn3(near, 2)
    col_arrived(3)
    scaled_grad(ring(zh, 3) * 2 + 1 - core)
    scaled_grad(ring(zh, 1) * 2 + 1 - core)
    turn3(far, 3)
    turn3(far, 1)
    col_arrived(1)
    col_send(2, 7, sibling)
    col_send(2, 8, sibling)
    scaled_grad(ring(zh, 2) * 2 + core)
    turn3(far, 2)
    col_arrived(4)
    scaled_grad(ring(zh, 2) * 2 + 1 - core)
    load.wait()
    table.wait()
    acc[...] = jnp.zeros_like(acc)
    products(0, 0, 128, G, R, 0)
    spread(0, 128)

    def ahead_of(zu):
        return 1 + 2 * zu

    def behind_of(zu):
        return 3 - 2 * zu

    def sum_send(kind, q, zu, o):
        first, second = places[q]
        step = behind_of(zu) if kind == 1 else ahead_of(zu)
        if kind == 2:
            src = c1.at[q, zu, o]
        else:
            src = unit(D, q, zu, first[o], second[2] if kind == 0 else along(second, step))
        i = o if kind == 0 else 4 + o
        send(src, (b1, b2, b3)[kind].at[q, zu, o], send_sem.at[2], sum_r.at[i], device(q, 1, step))

    def sum_arrived(i, tiles):
        arrived(D.at[pl.ds(0, tiles)], send_sem.at[2], sum_r.at[i], sibling)

    def sum_send2(kind, q, zu):
        step = behind_of(zu) if kind == 1 else ahead_of(zu)
        src = (e1.at[q, zu, 2], e1.at[q, zu, step], xc.at[q, zu])[kind]
        i = 8 if kind == 0 else 9 + zu
        send(src, (x1, x2, x3)[kind].at[q, zu], send_sem.at[2], sum_r.at[i], device(q, 0, step))

    def own_unit(q, zu, o, step):
        first, second = places[q]
        return unit(D, q, zu, first[o], along(second, step))[...].astype(F32)

    order = (2, 1, 3, 0)
    both = [(q, zu) for zu in (far, near) for q in halves]
    for kind in (0, 1):
        for o in order:
            for q, zu in both:
                sum_send(kind, q, zu, o)

    gathered(13, 32)

    def relay(o):
        sum_arrived(o, 8)
        for q, zu in both:
            c1[q, zu, o] = (b1[q, zu, o].astype(F32) + own_unit(q, zu, o, ahead_of(zu))).astype(BF16)
            sum_send(2, q, zu, o)

    def total1(o):
        sum_arrived(4 + o, 16)
        for q, zu in both:
            e1[q, zu, o] = (
                own_unit(q, zu, o, 0) + b2[q, zu, o].astype(F32) + b3[q, zu, o].astype(F32)
            ).astype(BF16)

    acc[...] = jnp.zeros_like(acc)
    products(8, 0, 64, X, Q, 1)
    relay(2)
    products(8, 64, 96, X, Q, 1)
    relay(1)
    products(8, 96, 128, X, Q, 1)

    def scaled(i, carry):
        F[i] = (rscale[i] * segment(8, Q, i)).astype(BF16)
        return carry

    lax.fori_loop(0, 32, scaled, 0, unroll=4)

    def fsum_send(kind, h):
        step = (1 if h == 0 else 3) if kind != 1 else (3 if h == 0 else 1)
        src = (he.at[ring(zh, 2), pl.ds(2 * h, 2)], he.at[ring(zh, step), pl.ds(2 * h, 2)], uc.at[h])[kind]
        send(src, (u1, u2, u3)[kind].at[h], send_sem.at[3], fsum_r.at[2 if kind == 0 else 3], on_zh(step))

    def fsum_arrived(i, tiles):
        arrived(F.at[pl.ds(0, tiles)], send_sem.at[3], fsum_r.at[i], sibling)

    for d in order:
        owner = ring(zh, d)
        send(shard(F, owner, 1 - core), h1.at[owner], send_sem.at[3], fsum_r.at[0 if d == 2 else 1], sibling)

    relay(3)
    w0[...] = jnp.zeros_like(w0)
    for owner in range(8):

        def share(k, carry):
            w0[...] += lax.dot_general(
                F[4 * owner + k],
                C[owner, pl.ds(pl.multiple_of(k * T, T), T), :],
                (((0,), (0,)), ((), ())),
                preferred_element_type=F32,
            )
            return carry

        lax.fori_loop(0, 4, share, 0, unroll=True)

    def ar_send(i, src, dst, device):
        send(src, dst, send_sem.at[4 if i in (0, 5) else 5], ar_r.at[i], device)

    def ar_arrived(i, dst):
        arrived(dst, send_sem.at[4], ar_r.at[i], sibling)

    def on_z_place(d):
        return lax.rem(z + d, 8)

    ar_send(0, w0.at[pl.ds((1 - core) * 64, 64)], a1, sibling)
    relay(0)
    fsum_arrived(0, 4)
    fsum_arrived(1, 12)
    for d in order:
        owner = ring(zh, d)
        he[owner] = (h1[owner].astype(F32) + shard(F, owner, core)[...].astype(F32)).astype(BF16)
        if d == 2:
            fsum_send(0, 0)
            fsum_send(0, 1)
    fsum_send(1, 0)
    fsum_send(1, 1)
    ar_arrived(0, a1)
    s1[...] = a1[...] + w0[pl.ds(core * 64, 64), :]
    for d in range(1, 8):
        ar_send(1, s1.at[pl.ds(on_z_place(d) * 8, 8)], a2.at[d - 1], on_z(d))
    fsum_arrived(2, 4)
    for h in halves:
        step = 1 if h == 0 else 3
        uc[h] = (u1[h].astype(F32) + he[ring(zh, step), pl.ds(2 * h, 2)].astype(F32)).astype(BF16)
        fsum_send(2, h)
    ar_arrived(1, a2)
    a3[y] = s1[pl.ds(z * 8, 8), :] + ((a2[0] + a2[1]) + (a2[2] + a2[3])) + ((a2[4] + a2[5]) + a2[6])
    for d in (1, 2, 3):
        ar_send(2, a3.at[y], a3.at[y], on_y[d])
    total1(2)
    for q, zu in both:
        sum_send2(0, q, zu)
    total1(1)
    total1(3)
    for q, zu in both:
        sum_send2(1, q, zu)
    ar_arrived(2, a2.at[pl.ds(0, 3)])
    a4[x] = (a3[0] + a3[1]) + (a3[2] + a3[3])
    for d in (1, 2, 3):
        ar_send(3, a4.at[x], a4.at[x], on_x[d])
    sum_arrived(8, 8)
    for q, zu in both:
        xc[q, zu] = (x1[q, zu].astype(F32) + e1[q, zu, ahead_of(zu)].astype(F32)).astype(BF16)
        sum_send2(2, q, zu)
    total1(0)

    fsum_arrived(3, 8)
    for n in range(4):
        h, k = n // 2, n % 2
        hidden = he[zh, n].astype(F32) + u2[h, k].astype(F32) + u3[h, k].astype(F32)
        rows = pl.ds(n * T, T)
        lo[rows, :] = jnp.dot(hidden.astype(BF16), we[...], preferred_element_type=F32).astype(BF16)
    outs = [pltpu.make_async_copy(lo, out_ref, out_sem.at[0])]
    outs[0].start()
    ar_arrived(3, a2.at[pl.ds(0, 3)])
    mine = pl.ds(core * 64 + z * 8, 8)
    full[mine, :] = (a4[0] + a4[1]) + (a4[2] + a4[3])
    for d in range(1, 8):
        ar_send(4, full.at[mine], full.at[mine], on_z(d))

    def total2(q, zu):
        return e1[q, zu, 0].astype(F32) + x2[q, zu].astype(F32) + x3[q, zu].astype(F32)

    sum_arrived(9 + far, 8)
    for q in halves:
        e2[q] = total2(q, far).astype(BF16)
        send(e2.at[q], bz.at[q], send_sem.at[2], sum_r.at[11], partner)
    ar_arrived(4, a2)
    half = full.at[pl.ds(core * 64, 64)]
    ar_send(5, half, half, sibling)
    ar_arrived(5, a1)
    outs.append(pltpu.make_async_copy(full, gw_ref, out_sem.at[1]))
    outs[1].start()
    sum_arrived(9 + near, 8)
    sum_arrived(11, 4)
    for q in halves:
        mine = total2(q, near) + bz[q].astype(F32)
        for k in (0, 1):
            n = 2 * q + k
            gi[pl.ds(n * T, T), :] = (cscale[n] * mine[k]).astype(BF16)
    outs.append(pltpu.make_async_copy(gi, gin_ref, out_sem.at[2]))
    outs[2].start()

    sent(X.at[pl.ds(0, 124)], send_sem.at[0], row_r.at[0], sibling)
    sent(C.at[pl.ds(0, 7)], send_sem.at[1], col_r.at[0], sibling)
    sent(D.at[pl.ds(0, 124)], send_sem.at[2], sum_r.at[0], sibling)
    sent(F.at[pl.ds(0, 28)], send_sem.at[3], fsum_r.at[0], sibling)
    sent(w0, send_sem.at[4], ar_r.at[0], sibling)
    sent(pad, send_sem.at[5], ar_r.at[0], sibling)
    for copy in outs:
        copy.wait()


def leave(*refs):
    n = len(refs) // 2
    for src, dst in zip(refs[:n], refs[n:]):
        dst[...] = src[...]


def body(features, weight, cotangent, tile_values, tile_coords, tile_count, row_degree, col_degree):
    units = lambda *lead: pltpu.VMEM((*lead, 2, T, T), BF16)
    sems = lambda n: pltpu.SemaphoreType.DMA((n,))
    rows = lambda n: pltpu.VMEM((n, T), F32)
    vmem = pl.BlockSpec(memory_space=pltpu.VMEM)
    anywhere = pl.BlockSpec(memory_space=pl.ANY)
    outs = (
        jax.ShapeDtypeStruct((512, T), BF16),
        jax.ShapeDtypeStruct((512, T), BF16),
        jax.ShapeDtypeStruct((T, T), F32),
    )
    results = pl.pallas_call(
        kernel,
        out_shape=outs,
        in_specs=[anywhere] * 5 + [pl.BlockSpec(memory_space=pltpu.SMEM), anywhere, anywhere],
        out_specs=(anywhere,) * 3,
        scratch_shapes=[
            pltpu.VMEM((128, T, T), BF16),
            pltpu.VMEM((128, T, T), BF16),
            pltpu.VMEM((8, 528, T), BF16),
            pltpu.VMEM((32, T, T), BF16),
            pltpu.VMEM((128, T, T), BF16),
            pltpu.VMEM((128, T, T), BF16),
            pltpu.VMEM((128, T, T), F32),
            pltpu.VMEM((32, T, T), BF16),
            rows(T),
            pltpu.VMEM((16, T), jnp.int32),
            pltpu.SMEM((16, T), jnp.int32),
            pltpu.VMEM((4, T, T), F32),
            pltpu.VMEM((32, T, T), F32),
            pltpu.VMEM((512, T), BF16),
            pltpu.VMEM((T, T), BF16),
            pltpu.VMEM((2, T), jnp.int32),
            pltpu.VMEM((4, T), jnp.int32),
            pltpu.VMEM((4, T), jnp.int32),
            pltpu.VMEM((512, T), BF16),
            pltpu.VMEM((512, T), BF16),
            units(2, 2, 4), units(2, 2, 4), units(2, 2, 4), units(2, 2, 4), units(2, 2, 4),
            units(2, 2), units(2, 2), units(2, 2), units(2, 2), units(2), units(2),
            pltpu.VMEM((4, 4, T, T), BF16),
            pltpu.VMEM((4, 4, T, T), BF16),
            units(2), units(2), units(2), units(2),
            rows(T),
            rows(64),
            pltpu.VMEM((7, 8, T), F32),
            pltpu.VMEM((4, 8, T), F32),
            pltpu.VMEM((4, 8, T), F32),
            rows(64),
            rows(T),
            rows(160),
            pltpu.SemaphoreType.DMA, sems(6), sems(3), pltpu.SemaphoreType.DMA,
            sems(6), sems(14), sems(12), sems(5), sems(4), sems(6),
        ],
        compiler_params=pltpu.CompilerParams(
            collective_id=0, has_side_effects=True, vmem_limit_bytes=60 * 1024 * 1024
        ),
    )(
        features,
        weight,
        cotangent,
        tile_values[0, 0],
        tile_coords[0, 0].T,
        tile_count,
        row_degree.reshape(4, T),
        col_degree.reshape(4, T),
    )
    return pl.pallas_call(
        leave,
        out_shape=outs,
        in_specs=[vmem] * 3,
        out_specs=(vmem,) * 3,
    )(*results)


def solution(mesh):
    in_specs = (
        P(("col", "row"), None),
        P(),
        P(("row", "col"), None),
        P("row", "col", None, None, None),
        P("row", "col", None, None),
        P("row", "col"),
        P(("row", "col")),
        P(("col", "row")),
    )
    out_specs = (P(("row", "col"), None), P(("col", "row"), None), P())
    return jax.shard_map(body, mesh=mesh, in_specs=in_specs, out_specs=out_specs, check_vma=False)
```

```python
import jax
import jax.numpy as jnp
from jax import lax
from jax.experimental import pallas as pl
from jax.experimental.pallas import tpu as pltpu
from jax.sharding import PartitionSpec as P

MESH = pl.DeviceIdType.MESH
T = 128
F32 = jnp.float32
BF16 = jnp.bfloat16


def ring(place, step):
    return lax.rem(place + step, 4)


def send(src, dst, ssem, rsem, device):
    pltpu.make_async_remote_copy(
        src_ref=src, dst_ref=dst, send_sem=ssem, recv_sem=rsem, device_id=device, device_id_type=MESH
    ).start()


def sent(src, ssem, rsem, device):
    pltpu.make_async_remote_copy(
        src_ref=src, dst_ref=src, send_sem=ssem, recv_sem=rsem, device_id=device, device_id_type=MESH
    ).wait_send()


def arrived(dst, ssem, rsem, device):
    pltpu.make_async_remote_copy(
        src_ref=dst, dst_ref=dst, send_sem=ssem, recv_sem=rsem, device_id=device, device_id_type=MESH
    ).wait_recv()


def kernel(
    feat, weight, cot, values, coords, count, rdeg, cdeg, out_ref, gin_ref, gw_ref,
    cn, X, V, C, G, D, R, Q, F, acc, vtab, stab, cscale, rscale, fe, we, co, rd, cd, lo, gi,
    b1, b2, b3, c1, e1, x1, x2, x3, xc, e2, bz,
    h1, he, u1, u2, u3, uc,
    w0, a1, a2, a3, a4, s1, full, pad,
    load_sem, in_sem, out_sem, tab_sem, send_sem, row_r, sum_r, col_r, fsum_r, ar_r,
):
    r, c = lax.axis_index("row"), lax.axis_index("col")
    zl, y, x = r // 16, lax.rem(r // 4, 4), lax.rem(r, 4)
    zh, core = c // 2, lax.rem(c, 2)
    z = zh * 2 + zl

    px, py = [ring(x, d) for d in range(4)], [ring(y, d) for d in range(4)]
    on_x = [(zl * 16 + y * 4 + px[d], c) for d in range(4)]
    on_y = [(zl * 16 + py[d] * 4 + x, c) for d in range(4)]
    places = ((px, py), (py, px))
    devices = ((on_x, on_y), (on_y, on_x))

    def along(items, step):
        if isinstance(step, int):
            return items[step]
        return jnp.where(step == 1, items[1], items[3])

    def device(q, axis, step):
        there = devices[q][axis]
        if isinstance(step, int):
            return there[step]
        return (jnp.where(step == 1, there[1][0], there[3][0]), c)

    def unit(ref, q, zu, p1, p2):
        i, j = (p1, p2) if q == 0 else (p2, p1)
        return ref.at[pl.ds(64 * zu + 16 * j + 4 * i + 2 * q, 2)]

    def on_zh(step):
        return (r, ring(zh, step) * 2 + core)

    def on_z(step):
        other = lax.rem(z + step, 8)
        return (lax.rem(other, 2) * 16 + y * 4 + x, (other // 2) * 2 + core)

    partner = ((1 - zl) * 16 + y * 4 + x, c)
    sibling = (r, zh * 2 + 1 - core)
    near, far = zl, 1 - zl
    halves = (0, 1)

    ins = [
        pltpu.make_async_copy(src, dst, in_sem.at[i])
        for i, (src, dst) in enumerate(
            ((cdeg, cd), (feat, fe), (rdeg, rd), (cot, C.at[c, pl.ds(0, 512)]), (weight, we), (coords, co), (count, cn))
        )
    ]
    for copy in ins:
        copy.start()
    load = pltpu.make_async_copy(values, V, load_sem)
    load.start()

    barrier = pltpu.get_barrier_semaphore()
    friends = [sibling]
    friends += [on_x[d] for d in (1, 2, 3)]
    friends += [on_y[d] for d in (1, 2, 3)]
    friends += [on_z(d) for d in range(1, 8)]
    for friend in friends:
        pl.semaphore_signal(barrier, inc=1, device_id=friend, device_id_type=MESH)

    def column(line):
        return jnp.transpose(jnp.broadcast_to(1.0 / jnp.sqrt(line.astype(F32)), (T, T)))

    for copy in ins:
        copy.wait()
    for k in range(4):
        cscale[k] = column(cd[k : k + 1, :])
        X[4 * r + k] = (fe[pl.ds(k * T, T), :].astype(F32) * cscale[k]).astype(BF16)
    line = lax.broadcasted_iota(jnp.int32, (16, T), 0)
    tail = jnp.ones((16, T), F32)
    for k in range(4):
        tail = jnp.where(line == k, jnp.broadcast_to(rd[k : k + 1, :].astype(F32), (16, T)), tail)
    C[c, pl.ds(512, 16), :] = tail.astype(BF16)

    pl.semaphore_wait(barrier, len(friends))

    def route(zu, k):
        if k == 0:
            return 0, 1
        if k == 1:
            return 0, 3
        return 3 - 2 * zu, 1 + 2 * zu

    def gather1(q, zu, k):
        first, second = places[q]
        back, ahead = route(zu, k)
        piece = unit(X, q, zu, along(first, back), second[0])
        send(piece, piece, send_sem.at[0], row_r.at[6 * zu + k // 2], device(q, 0, ahead))

    def gather2(q, zu, o, k):
        first, second = places[q]
        back, ahead = route(zu, k)
        piece = unit(X, q, zu, first[o], along(second, back))
        i = 13 if k == 2 else 6 * zu + 2 + o
        send(piece, piece, send_sem.at[0], row_r.at[i], device(q, 1, ahead))

    def gathered(i, tiles):
        arrived(X.at[pl.ds(0, tiles)], send_sem.at[0], row_r.at[i], sibling)

    def shard(ref, zh_of, core_of):
        return ref.at[pl.ds(4 * (zh_of * 2 + core_of), 4)]

    def col_piece(owner_step, i, core_of):
        whose = ring(zh, owner_step) * 2 + core_of
        if i in (2, 7):
            return C.at[whose, pl.ds(0, 256)]
        if i in (3, 8):
            return C.at[whose, pl.ds(256, 272)]
        return C.at[whose]

    def col_send(owner_step, i, device):
        piece = col_piece(owner_step, i, core)
        send(piece, piece, send_sem.at[1], col_r.at[(0, 0, 1, 1, 2, 3, 3, 4, 4)[i]], device)

    def col_arrived(i):
        n = (2, 1, 1, 2, 1)[i]
        arrived(C.at[pl.ds(0, n)], send_sem.at[1], col_r.at[i], sibling)

    def scaled_grad(owner):
        lines = C[owner, pl.ds(512, 16), :].astype(F32)
        for k in range(4):
            n = 4 * owner + k
            scale = column(lines[k : k + 1, :])
            rscale[n] = scale
            grad = lax.dot_general(
                C[owner, pl.ds(k * T, T), :], we[...], (((1,), (1,)), ((), ())), preferred_element_type=F32
            )
            G[n] = (scale * grad).astype(BF16)

    for q in halves:
        piece = unit(X, q, near, places[q][0][0], places[q][1][0])
        send(piece, piece, send_sem.at[0], row_r.at[12], partner)
    for q in halves:
        gather1(q, near, 0)
        gather1(q, near, 1)
    for q in halves:
        gather2(q, near, 0, 0)
        gather2(q, near, 0, 1)
    col_send(0, 0, on_zh(1))
    col_send(0, 1, on_zh(3))
    col_send(0, 4, sibling)

    own = lax.broadcasted_iota(jnp.int32, (T, T), 0)
    lane = lax.broadcasted_iota(jnp.int32, (T, T), 1)
    live = own < jnp.broadcast_to(cn[...], (T, T))
    by_row = jnp.transpose(jnp.broadcast_to(co[0:1, :], (T, T)))
    by_col = jnp.transpose(jnp.broadcast_to(co[1:2, :], (T, T)))
    def pick(mask, what):
        return jnp.sum(jnp.where(mask, what, 0), axis=0, keepdims=True)

    for base, major, other in ((0, by_col, by_row), (8, by_row, by_col)):
        major = jnp.where(live, major, T)
        key = major * T + own
        rank = pick(key < jnp.transpose(key), jnp.ones_like(key))
        rank = jnp.transpose(jnp.broadcast_to(rank, (T, T)))
        here = rank == lane
        target = pick(here, major)
        before = pick(rank + 1 == lane, major + 1) - 1
        vtab[base : base + 1, :] = pick(here, own)
        vtab[base + 1 : base + 2, :] = pick(here, other)
        vtab[base + 2 : base + 3, :] = (target == before).astype(jnp.int32)
        vtab[base + 3 : base + 4, :] = jnp.maximum(pick(major <= lane, jnp.ones_like(key)) - 1, 0)
        vtab[base + 4 : base + 5, :] = jnp.minimum(pick(major == lane, jnp.ones_like(key)), 1)
    table = pltpu.make_async_copy(vtab, stab, tab_sem)
    table.start()

    def products(base, first, last, source, out, contract):
        def step(k, carry):
            tile = V[stab[base, k]]
            rows = source[stab[base + 1, k]]
            prod = lax.dot_general(tile, rows, (((contract,), (0,)), ((), ())), preferred_element_type=F32)
            total = prod + jnp.where(stab[base + 2, k] == 1, acc[...], 0.0)
            acc[...] = total
            out[k] = total.astype(out.dtype)
            return carry

        lax.fori_loop(first, last, step, 0, unroll=4)

    def segment(base, segments, j):
        return jnp.where(stab[base + 4, j] == 1, segments[stab[base + 3, j]], 0.0)

    def spread(first, last):
        def step(j, carry):
            D[j] = segment(0, R, j).astype(BF16)
            return carry

        lax.fori_loop(first, last, step, 0, unroll=4)

    def turn1(zu):
        gathered(6 * zu, 8)
        for q in halves:
            gather1(q, zu, 2)
        for o in (3, 1):
            for q in halves:
                gather2(q, zu, o, 0)
                gather2(q, zu, o, 1)

    def turn2(zu):
        gathered(6 * zu + 1, 4)
        for q in halves:
            gather2(q, zu, 2, 0)
            gather2(q, zu, 2, 1)

    def turn3(zu, o):
        gathered(6 * zu + 2 + o, 8)
        for q in halves:
            gather2(q, zu, o, 2)

    turn1(near)
    gathered(12, 4)
    for q in halves:
        gather1(q, far, 0)
        gather1(q, far, 1)
    for q in halves:
        gather2(q, far, 0, 0)
        gather2(q, far, 0, 1)
    turn2(near)
    turn3(near, 0)
    scaled_grad(c)
    col_arrived(2)
    scaled_grad(zh * 2 + 1 - core)
    turn1(far)
    turn3(near, 3)
    turn3(near, 1)
    col_arrived(0)
    col_send(3, 2, on_zh(1))
    col_send(1, 3, on_zh(3))
    col_send(3, 5, sibling)
    col_send(1, 6, sibling)
    turn3(far, 0)
    scaled_grad(ring(zh, 3) * 2 + core)
    scaled_grad(ring(zh, 1) * 2 + core)
    turn3(near, 2)
    turn2(far)
    col_arrived(3)
    scaled_grad(ring(zh, 3) * 2 + 1 - core)
    scaled_grad(ring(zh, 1) * 2 + 1 - core)
    col_arrived(1)
    col_send(2, 7, sibling)
    col_send(2, 8, sibling)
    scaled_grad(ring(zh, 2) * 2 + core)
    col_arrived(4)
    scaled_grad(ring(zh, 2) * 2 + 1 - core)
    load.wait()
    table.wait()
    acc[...] = jnp.zeros_like(acc)
    products(0, 0, 48, G, R, 0)
    turn3(far, 3)
    turn3(far, 1)
    products(0, 48, 128, G, R, 0)
    turn3(far, 2)
    spread(0, 128)

    def ahead_of(zu):
        return 1 + 2 * zu

    def behind_of(zu):
        return 3 - 2 * zu

    def sum_send(kind, q, zu, o):
        first, second = places[q]
        step = behind_of(zu) if kind == 1 else ahead_of(zu)
        if kind == 2:
            src = c1.at[q, zu, o]
        else:
            src = unit(D, q, zu, first[o], second[2] if kind == 0 else along(second, step))
        i = o if kind == 0 else 4 + o
        send(src, (b1, b2, b3)[kind].at[q, zu, o], send_sem.at[2], sum_r.at[i], device(q, 1, step))

    def sum_arrived(i, tiles):
        arrived(D.at[pl.ds(0, tiles)], send_sem.at[2], sum_r.at[i], sibling)

    def sum_send2(kind, q, zu):
        step = behind_of(zu) if kind == 1 else ahead_of(zu)
        src = (e1.at[q, zu, 2], e1.at[q, zu, step], xc.at[q, zu])[kind]
        i = 8 if kind == 0 else 9 + zu
        send(src, (x1, x2, x3)[kind].at[q, zu], send_sem.at[2], sum_r.at[i], device(q, 0, step))

    def own_unit(q, zu, o, step):
        first, second = places[q]
        return unit(D, q, zu, first[o], along(second, step))[...].astype(F32)

    order = (2, 1, 3, 0)
    both = [(q, zu) for zu in (far, near) for q in halves]
    for kind in (0, 1):
        for o in order:
            for q, zu in both:
                sum_send(kind, q, zu, o)

    gathered(13, 32)

    def relay(o):
        sum_arrived(o, 8)
        for q, zu in both:
            c1[q, zu, o] = (b1[q, zu, o].astype(F32) + own_unit(q, zu, o, ahead_of(zu))).astype(BF16)
            sum_send(2, q, zu, o)

    def total1(o):
        sum_arrived(4 + o, 16)
        for q, zu in both:
            e1[q, zu, o] = (
                own_unit(q, zu, o, 0) + b2[q, zu, o].astype(F32) + b3[q, zu, o].astype(F32)
            ).astype(BF16)

    acc[...] = jnp.zeros_like(acc)
    products(8, 0, 48, X, Q, 1)
    relay(2)
    products(8, 48, 88, X, Q, 1)
    relay(1)
    products(8, 88, 128, X, Q, 1)
    relay(3)

    def scaled(i, carry):
        F[i] = (rscale[i] * segment(8, Q, i)).astype(BF16)
        return carry

    lax.fori_loop(0, 32, scaled, 0, unroll=4)

    def fsum_send(kind, h):
        step = (1 if h == 0 else 3) if kind != 1 else (3 if h == 0 else 1)
        src = (he.at[ring(zh, 2), pl.ds(2 * h, 2)], he.at[ring(zh, step), pl.ds(2 * h, 2)], uc.at[h])[kind]
        send(src, (u1, u2, u3)[kind].at[h], send_sem.at[3], fsum_r.at[2 if kind == 0 else 3], on_zh(step))

    def fsum_arrived(i, tiles):
        arrived(F.at[pl.ds(0, tiles)], send_sem.at[3], fsum_r.at[i], sibling)

    for d in order:
        owner = ring(zh, d)
        send(shard(F, owner, 1 - core), h1.at[owner], send_sem.at[3], fsum_r.at[0 if d == 2 else 1], sibling)

    w0[...] = jnp.zeros_like(w0)
    for owner in range(8):

        def share(k, carry):
            w0[...] += lax.dot_general(
                F[4 * owner + k],
                C[owner, pl.ds(pl.multiple_of(k * T, T), T), :],
                (((0,), (0,)), ((), ())),
                preferred_element_type=F32,
            )
            return carry

        lax.fori_loop(0, 4, share, 0, unroll=True)

    def ar_send(i, src, dst, device):
        send(src, dst, send_sem.at[4 if i == 0 else 5], ar_r.at[i], device)

    def ar_arrived(i, dst):
        arrived(dst, send_sem.at[4], ar_r.at[i], sibling)

    def z_rows(step):
        return pl.ds(lax.rem(z + step, 8) * 16, 16)

    def relay2(q, zu):
        xc[q, zu] = (x1[q, zu].astype(F32) + e1[q, zu, ahead_of(zu)].astype(F32)).astype(BF16)
        sum_send2(2, q, zu)

    def total2(q, zu):
        return e1[q, zu, 0].astype(F32) + x2[q, zu].astype(F32) + x3[q, zu].astype(F32)

    ar_send(0, w0, a1, sibling)
    fsum_arrived(0, 4)
    fsum_arrived(1, 12)
    for d in order:
        owner = ring(zh, d)
        he[owner] = (h1[owner].astype(F32) + shard(F, owner, core)[...].astype(F32)).astype(BF16)
    ar_arrived(0, a1)
    s1[...] = a1[...] + w0[...]
    for d in range(1, 8):
        ar_send(1, s1.at[z_rows(d)], a2.at[d - 1], on_z(d))
    for kind in (0, 1):
        for h in halves:
            fsum_send(kind, h)
    ar_arrived(1, a2)
    a3[y] = s1[z_rows(0), :] + ((a2[0] + a2[1]) + (a2[2] + a2[3])) + ((a2[4] + a2[5]) + a2[6])
    for d in (1, 2, 3):
        ar_send(2, a3.at[y], a3.at[y], on_y[d])
    total1(2)
    for q, zu in both:
        sum_send2(0, q, zu)
    relay(0)
    fsum_arrived(2, 4)
    for h in halves:
        step = 1 if h == 0 else 3
        uc[h] = (u1[h].astype(F32) + he[ring(zh, step), pl.ds(2 * h, 2)].astype(F32)).astype(BF16)
        fsum_send(2, h)
    total1(1)
    total1(3)
    for q in halves:
        sum_send2(1, q, far)
    ar_arrived(2, a2.at[pl.ds(0, 3)])
    a4[x] = (a3[0] + a3[1]) + (a3[2] + a3[3])
    for d in (1, 2, 3):
        ar_send(3, a4.at[x], a4.at[x], on_x[d])
    sum_arrived(8, 8)
    for q in halves:
        relay2(q, far)
    for q in halves:
        sum_send2(1, q, near)
    for q in halves:
        relay2(q, near)
    total1(0)
    ar_arrived(3, a2.at[pl.ds(0, 3)])
    full[z_rows(0), :] = (a4[0] + a4[1]) + (a4[2] + a4[3])
    for d in range(1, 8):
        ar_send(4, full.at[z_rows(0)], full.at[z_rows(0)], on_z(d))
    sum_arrived(9 + far, 8)
    for q in halves:
        e2[q] = total2(q, far).astype(BF16)
        send(e2.at[q], bz.at[q], send_sem.at[2], sum_r.at[11], partner)

    fsum_arrived(3, 8)
    for n in range(4):
        h, k = n // 2, n % 2
        hidden = he[zh, n].astype(F32) + u2[h, k].astype(F32) + u3[h, k].astype(F32)
        rows = pl.ds(n * T, T)
        lo[rows, :] = jnp.dot(hidden.astype(BF16), we[...], preferred_element_type=F32).astype(BF16)
    outs = [pltpu.make_async_copy(lo, out_ref, out_sem.at[0])]
    outs[0].start()
    ar_arrived(4, a2)
    outs.append(pltpu.make_async_copy(full, gw_ref, out_sem.at[1]))
    outs[1].start()
    sum_arrived(9 + near, 8)
    sum_arrived(11, 4)
    for q in halves:
        mine = total2(q, near) + bz[q].astype(F32)
        for k in (0, 1):
            n = 2 * q + k
            gi[pl.ds(n * T, T), :] = (cscale[n] * mine[k]).astype(BF16)
    outs.append(pltpu.make_async_copy(gi, gin_ref, out_sem.at[2]))
    outs[2].start()

    sent(X.at[pl.ds(0, 124)], send_sem.at[0], row_r.at[0], sibling)
    sent(C.at[pl.ds(0, 7)], send_sem.at[1], col_r.at[0], sibling)
    sent(D.at[pl.ds(0, 124)], send_sem.at[2], sum_r.at[0], sibling)
    sent(F.at[pl.ds(0, 28)], send_sem.at[3], fsum_r.at[0], sibling)
    sent(w0, send_sem.at[4], ar_r.at[0], sibling)
    sent(pad, send_sem.at[5], ar_r.at[0], sibling)
    for copy in outs:
        copy.wait()


def leave(*refs):
    n = len(refs) // 2
    for src, dst in zip(refs[:n], refs[n:]):
        dst[...] = src[...]


def body(features, weight, cotangent, tile_values, tile_coords, tile_count, row_degree, col_degree):
    units = lambda *lead: pltpu.VMEM((*lead, 2, T, T), BF16)
    sems = lambda n: pltpu.SemaphoreType.DMA((n,))
    rows = lambda n: pltpu.VMEM((n, T), F32)
    vmem = pl.BlockSpec(memory_space=pltpu.VMEM)
    anywhere = pl.BlockSpec(memory_space=pl.ANY)
    outs = (
        jax.ShapeDtypeStruct((512, T), BF16),
        jax.ShapeDtypeStruct((512, T), BF16),
        jax.ShapeDtypeStruct((T, T), F32),
    )
    results = pl.pallas_call(
        kernel,
        out_shape=outs,
        in_specs=[anywhere] * 8,
        out_specs=(anywhere,) * 3,
        scratch_shapes=[
            pltpu.VMEM((1, 1), jnp.int32),
            pltpu.VMEM((128, T, T), BF16),
            pltpu.VMEM((128, T, T), BF16),
            pltpu.VMEM((8, 528, T), BF16),
            pltpu.VMEM((32, T, T), BF16),
            pltpu.VMEM((128, T, T), BF16),
            pltpu.VMEM((128, T, T), BF16),
            pltpu.VMEM((128, T, T), F32),
            pltpu.VMEM((32, T, T), BF16),
            rows(T),
            pltpu.VMEM((16, T), jnp.int32),
            pltpu.SMEM((16, T), jnp.int32),
            pltpu.VMEM((4, T, T), F32),
            pltpu.VMEM((32, T, T), F32),
            pltpu.VMEM((512, T), BF16),
            pltpu.VMEM((T, T), BF16),
            pltpu.VMEM((2, T), jnp.int32),
            pltpu.VMEM((4, T), jnp.int32),
            pltpu.VMEM((4, T), jnp.int32),
            pltpu.VMEM((512, T), BF16),
            pltpu.VMEM((512, T), BF16),
            units(2, 2, 4), units(2, 2, 4), units(2, 2, 4), units(2, 2, 4), units(2, 2, 4),
            units(2, 2), units(2, 2), units(2, 2), units(2, 2), units(2), units(2),
            pltpu.VMEM((4, 4, T, T), BF16),
            pltpu.VMEM((4, 4, T, T), BF16),
            units(2), units(2), units(2), units(2),
            rows(T),
            rows(T),
            pltpu.VMEM((7, 16, T), F32),
            pltpu.VMEM((4, 16, T), F32),
            pltpu.VMEM((4, 16, T), F32),
            rows(T),
            rows(T),
            rows(320),
            pltpu.SemaphoreType.DMA, sems(7), sems(3), pltpu.SemaphoreType.DMA,
            sems(6), sems(14), sems(12), sems(5), sems(4), sems(6),
        ],
        compiler_params=pltpu.CompilerParams(
            collective_id=0, has_side_effects=True, vmem_limit_bytes=60 * 1024 * 1024
        ),
    )(
        features,
        weight,
        cotangent,
        tile_values[0, 0],
        tile_coords[0, 0].T,
        tile_count,
        row_degree.reshape(4, T),
        col_degree.reshape(4, T),
    )
    return pl.pallas_call(
        leave,
        out_shape=outs,
        in_specs=[vmem] * 3,
        out_specs=(vmem,) * 3,
    )(*results)


def solution(mesh):
    in_specs = (
        P(("col", "row"), None),
        P(),
        P(("row", "col"), None),
        P("row", "col", None, None, None),
        P("row", "col", None, None),
        P("row", "col"),
        P(("row", "col")),
        P(("col", "row")),
    )
    out_specs = (P(("row", "col"), None), P(("col", "row"), None), P())
    return jax.shard_map(body, mesh=mesh, in_specs=in_specs, out_specs=out_specs, check_vma=False)
```

```python
import jax
import jax.numpy as jnp
from jax import lax
from jax.experimental import pallas as pl
from jax.experimental.pallas import tpu as pltpu
from jax.sharding import PartitionSpec as P

MESH = pl.DeviceIdType.MESH
T = 128
F32 = jnp.float32
BF16 = jnp.bfloat16


def ring(place, step):
    return lax.rem(place + step, 4)


def send(src, dst, ssem, rsem, device):
    pltpu.make_async_remote_copy(
        src_ref=src, dst_ref=dst, send_sem=ssem, recv_sem=rsem, device_id=device, device_id_type=MESH
    ).start()


def sent(src, ssem, rsem, device):
    pltpu.make_async_remote_copy(
        src_ref=src, dst_ref=src, send_sem=ssem, recv_sem=rsem, device_id=device, device_id_type=MESH
    ).wait_send()


def arrived(dst, ssem, rsem, device):
    pltpu.make_async_remote_copy(
        src_ref=dst, dst_ref=dst, send_sem=ssem, recv_sem=rsem, device_id=device, device_id_type=MESH
    ).wait_recv()


def kernel(
    feat, weight, cot, values, coords, count, rdeg, cdeg, out_ref, gin_ref, gw_ref,
    cn, X, V, C, G, D, R, Q, F, acc, vtab, stab, cscale, rscale, fe, we, co, rd, cd, lo, gi,
    b1, b2, b3, c1, e1, x1, x2, x3, xc, e2, bz,
    h1, he, u1, u2, u3, uc,
    w0, a1, a2, a3, a4, s1, full, pad,
    load_sem, in_sem, out_sem, tab_sem, send_sem, row_r, sum_r, col_r, fsum_r, ar_r,
):
    r, c = lax.axis_index("row"), lax.axis_index("col")
    zl, y, x = r // 16, lax.rem(r // 4, 4), lax.rem(r, 4)
    zh, core = c // 2, lax.rem(c, 2)
    z = zh * 2 + zl

    px, py = [ring(x, d) for d in range(4)], [ring(y, d) for d in range(4)]
    on_x = [(zl * 16 + y * 4 + px[d], c) for d in range(4)]
    on_y = [(zl * 16 + py[d] * 4 + x, c) for d in range(4)]
    places = ((px, py), (py, px))
    devices = ((on_x, on_y), (on_y, on_x))

    def along(items, step):
        if isinstance(step, int):
            return items[step]
        return jnp.where(step == 1, items[1], items[3])

    def device(q, axis, step):
        there = devices[q][axis]
        if isinstance(step, int):
            return there[step]
        return (jnp.where(step == 1, there[1][0], there[3][0]), c)

    def unit(ref, q, zu, p1, p2):
        i, j = (p1, p2) if q == 0 else (p2, p1)
        return ref.at[pl.ds(64 * zu + 16 * j + 4 * i + 2 * q, 2)]

    def on_zh(step):
        return (r, ring(zh, step) * 2 + core)

    def on_z(step):
        other = lax.rem(z + step, 8)
        return (lax.rem(other, 2) * 16 + y * 4 + x, (other // 2) * 2 + core)

    partner = ((1 - zl) * 16 + y * 4 + x, c)
    sibling = (r, zh * 2 + 1 - core)
    near, far = zl, 1 - zl
    halves = (0, 1)

    ins = [
        pltpu.make_async_copy(src, dst, in_sem.at[i])
        for i, (src, dst) in enumerate(
            ((cdeg, cd), (feat, fe), (rdeg, rd), (cot, C.at[c, pl.ds(0, 512)]), (weight, we), (coords, co), (count, cn))
        )
    ]
    for copy in ins:
        copy.start()
    load = pltpu.make_async_copy(values, V, load_sem)
    load.start()

    barrier = pltpu.get_barrier_semaphore()
    friends = [sibling]
    friends += [on_x[d] for d in (1, 2, 3)]
    friends += [on_y[d] for d in (1, 2, 3)]
    friends += [on_z(d) for d in range(1, 8)]
    for friend in friends:
        pl.semaphore_signal(barrier, inc=1, device_id=friend, device_id_type=MESH)

    def column(line):
        return jnp.transpose(jnp.broadcast_to(1.0 / jnp.sqrt(line.astype(F32)), (T, T)))

    for copy in ins:
        copy.wait()
    for k in range(4):
        cscale[k] = column(cd[k : k + 1, :])
        X[4 * r + k] = (fe[pl.ds(k * T, T), :].astype(F32) * cscale[k]).astype(BF16)
    line = lax.broadcasted_iota(jnp.int32, (16, T), 0)
    tail = jnp.ones((16, T), F32)
    for k in range(4):
        tail = jnp.where(line == k, jnp.broadcast_to(rd[k : k + 1, :].astype(F32), (16, T)), tail)
    C[c, pl.ds(512, 16), :] = tail.astype(BF16)

    pl.semaphore_wait(barrier, len(friends))

    def route(zu, k):
        if k == 0:
            return 0, 1
        if k == 1:
            return 0, 3
        return 3 - 2 * zu, 1 + 2 * zu

    def gather1(q, zu, k):
        first, second = places[q]
        back, ahead = route(zu, k)
        piece = unit(X, q, zu, along(first, back), second[0])
        send(piece, piece, send_sem.at[0], row_r.at[6 * zu + k // 2], device(q, 0, ahead))

    def gather2(q, zu, o, k):
        first, second = places[q]
        back, ahead = route(zu, k)
        piece = unit(X, q, zu, first[o], along(second, back))
        i = 13 if k == 2 else 6 * zu + 2 + o
        send(piece, piece, send_sem.at[0], row_r.at[i], device(q, 1, ahead))

    def gathered(i, tiles):
        arrived(X.at[pl.ds(0, tiles)], send_sem.at[0], row_r.at[i], sibling)

    def shard(ref, zh_of, core_of):
        return ref.at[pl.ds(4 * (zh_of * 2 + core_of), 4)]

    def col_piece(owner_step, i, core_of):
        whose = ring(zh, owner_step) * 2 + core_of
        if i in (2, 7):
            return C.at[whose, pl.ds(0, 256)]
        if i in (3, 8):
            return C.at[whose, pl.ds(256, 272)]
        return C.at[whose]

    def col_send(owner_step, i, device):
        piece = col_piece(owner_step, i, core)
        send(piece, piece, send_sem.at[1], col_r.at[(0, 0, 1, 1, 2, 3, 3, 4, 4)[i]], device)

    def col_arrived(i):
        n = (2, 1, 1, 2, 1)[i]
        arrived(C.at[pl.ds(0, n)], send_sem.at[1], col_r.at[i], sibling)

    def scaled_grad(owner):
        lines = C[owner, pl.ds(512, 16), :].astype(F32)
        for k in range(4):
            n = 4 * owner + k
            scale = column(lines[k : k + 1, :])
            rscale[n] = scale
            grad = lax.dot_general(
                C[owner, pl.ds(k * T, T), :], we[...], (((1,), (1,)), ((), ())), preferred_element_type=F32
            )
            G[n] = jnp.transpose((scale * grad).astype(BF16))

    for q in halves:
        piece = unit(X, q, near, places[q][0][0], places[q][1][0])
        send(piece, piece, send_sem.at[0], row_r.at[12], partner)
    for q in halves:
        gather1(q, near, 0)
        gather1(q, near, 1)
    for q in halves:
        gather2(q, near, 0, 0)
        gather2(q, near, 0, 1)
    col_send(0, 0, on_zh(1))
    col_send(0, 1, on_zh(3))
    col_send(0, 4, sibling)

    own = lax.broadcasted_iota(jnp.int32, (T, T), 0)
    lane = lax.broadcasted_iota(jnp.int32, (T, T), 1)
    live = own < jnp.broadcast_to(cn[...], (T, T))
    by_row = jnp.transpose(jnp.broadcast_to(co[0:1, :], (T, T)))
    by_col = jnp.transpose(jnp.broadcast_to(co[1:2, :], (T, T)))
    def pick(mask, what):
        return jnp.sum(jnp.where(mask, what, 0), axis=0, keepdims=True)

    for base, major, other in ((0, by_col, by_row), (8, by_row, by_col)):
        major = jnp.where(live, major, T)
        key = major * T + own
        rank = pick(key < jnp.transpose(key), jnp.ones_like(key))
        rank = jnp.transpose(jnp.broadcast_to(rank, (T, T)))
        here = rank == lane
        target = pick(here, major)
        before = pick(rank + 1 == lane, major + 1) - 1
        vtab[base : base + 1, :] = pick(here, own)
        vtab[base + 1 : base + 2, :] = pick(here, other)
        vtab[base + 2 : base + 3, :] = (target == before).astype(jnp.int32)
        vtab[base + 3 : base + 4, :] = jnp.maximum(pick(major <= lane, jnp.ones_like(key)) - 1, 0)
        vtab[base + 4 : base + 5, :] = jnp.minimum(pick(major == lane, jnp.ones_like(key)), 1)
    table = pltpu.make_async_copy(vtab, stab, tab_sem)
    table.start()

    def products(base, first, last, source, out, contract):
        def step(i, carry):
            total = acc[...]
            for k in range(8):
                k += 8 * i
                tile = V[stab[base, k]]
                rows = source[stab[base + 1, k]]
                pair = (tile, rows) if contract else (rows, tile)
                prod = jnp.dot(*pair, preferred_element_type=F32)
                total = prod + jnp.where(stab[base + 2, k] == 1, total, 0.0)
                out[k] = total.astype(out.dtype)
            acc[...] = total
            return carry

        lax.fori_loop(first // 8, last // 8, step, 0, unroll=1)

    def segment(base, segments, j):
        return jnp.where(stab[base + 4, j] == 1, segments[stab[base + 3, j]], 0.0)

    def spread(first, last):
        def step(j, carry):
            D[j] = segment(0, R, j).astype(BF16)
            return carry

        lax.fori_loop(first, last, step, 0, unroll=4)

    def turn1(zu):
        gathered(6 * zu, 8)
        for q in halves:
            gather1(q, zu, 2)
        for o in (3, 1):
            for q in halves:
                gather2(q, zu, o, 0)
                gather2(q, zu, o, 1)

    def turn2(zu):
        gathered(6 * zu + 1, 4)
        for q in halves:
            gather2(q, zu, 2, 0)
            gather2(q, zu, 2, 1)

    def turn3(zu, o):
        gathered(6 * zu + 2 + o, 8)
        for q in halves:
            gather2(q, zu, o, 2)

    turn1(near)
    gathered(12, 4)
    for q in halves:
        gather1(q, far, 0)
        gather1(q, far, 1)
    for q in halves:
        gather2(q, far, 0, 0)
        gather2(q, far, 0, 1)
    turn2(near)
    turn3(near, 0)
    scaled_grad(c)
    col_arrived(2)
    scaled_grad(zh * 2 + 1 - core)
    turn1(far)
    turn3(near, 3)
    turn3(near, 1)
    col_arrived(0)
    col_send(3, 2, on_zh(1))
    col_send(1, 3, on_zh(3))
    col_send(3, 5, sibling)
    col_send(1, 6, sibling)
    turn3(far, 0)
    scaled_grad(ring(zh, 3) * 2 + core)
    scaled_grad(ring(zh, 1) * 2 + core)
    turn3(near, 2)
    turn2(far)
    col_arrived(3)
    scaled_grad(ring(zh, 3) * 2 + 1 - core)
    scaled_grad(ring(zh, 1) * 2 + 1 - core)
    col_arrived(1)
    col_send(2, 7, sibling)
    col_send(2, 8, sibling)
    scaled_grad(ring(zh, 2) * 2 + core)
    col_arrived(4)
    scaled_grad(ring(zh, 2) * 2 + 1 - core)
    load.wait()
    table.wait()
    acc[...] = jnp.zeros_like(acc)
    products(0, 0, 48, G, R, 0)
    turn3(far, 3)
    turn3(far, 1)
    products(0, 48, 128, G, R, 0)
    turn3(far, 2)
    spread(0, 128)

    def ahead_of(zu):
        return 1 + 2 * zu

    def behind_of(zu):
        return 3 - 2 * zu

    def sum_send(kind, q, zu, o):
        first, second = places[q]
        step = behind_of(zu) if kind == 1 else ahead_of(zu)
        if kind == 2:
            src = c1.at[q, zu, o]
        else:
            src = unit(D, q, zu, first[o], second[2] if kind == 0 else along(second, step))
        i = o if kind == 0 else 4 + o
        send(src, (b1, b2, b3)[kind].at[q, zu, o], send_sem.at[2], sum_r.at[i], device(q, 1, step))

    def sum_arrived(i, tiles):
        arrived(D.at[pl.ds(0, tiles)], send_sem.at[2], sum_r.at[i], sibling)

    def sum_send2(kind, q, zu):
        step = behind_of(zu) if kind == 1 else ahead_of(zu)
        src = (e1.at[q, zu, 2], e1.at[q, zu, step], xc.at[q, zu])[kind]
        i = 8 if kind == 0 else 9 + zu
        send(src, (x1, x2, x3)[kind].at[q, zu], send_sem.at[2], sum_r.at[i], device(q, 0, step))

    def own_unit(q, zu, o, step):
        first, second = places[q]
        return unit(D, q, zu, first[o], along(second, step))[...].astype(F32)

    order = (2, 1, 3, 0)
    both = [(q, zu) for zu in (far, near) for q in halves]
    for kind in (0, 1):
        for o in order:
            for q, zu in both:
                sum_send(kind, q, zu, o)

    gathered(13, 32)

    def relay(o):
        sum_arrived(o, 8)
        for q, zu in both:
            c1[q, zu, o] = (b1[q, zu, o].astype(F32) + own_unit(q, zu, o, ahead_of(zu))).astype(BF16)
            sum_send(2, q, zu, o)

    def total1(o):
        sum_arrived(4 + o, 16)
        for q, zu in both:
            e1[q, zu, o] = (
                own_unit(q, zu, o, 0) + b2[q, zu, o].astype(F32) + b3[q, zu, o].astype(F32)
            ).astype(BF16)

    acc[...] = jnp.zeros_like(acc)
    products(8, 0, 48, X, Q, 1)
    relay(2)
    products(8, 48, 88, X, Q, 1)
    relay(1)
    products(8, 88, 128, X, Q, 1)
    relay(3)

    def scaled(i, carry):
        F[i] = (rscale[i] * segment(8, Q, i)).astype(BF16)
        return carry

    lax.fori_loop(0, 32, scaled, 0, unroll=4)

    def fsum_send(kind, h):
        step = (1 if h == 0 else 3) if kind != 1 else (3 if h == 0 else 1)
        src = (he.at[ring(zh, 2), pl.ds(2 * h, 2)], he.at[ring(zh, step), pl.ds(2 * h, 2)], uc.at[h])[kind]
        send(src, (u1, u2, u3)[kind].at[h], send_sem.at[3], fsum_r.at[2 if kind == 0 else 3], on_zh(step))

    def fsum_arrived(i, tiles):
        arrived(F.at[pl.ds(0, tiles)], send_sem.at[3], fsum_r.at[i], sibling)

    for d in order:
        owner = ring(zh, d)
        send(shard(F, owner, 1 - core), h1.at[owner], send_sem.at[3], fsum_r.at[0 if d == 2 else 1], sibling)

    w0[...] = jnp.zeros_like(w0)
    for owner in range(8):

        def share(k, carry):
            w0[...] += lax.dot_general(
                F[4 * owner + k],
                C[owner, pl.ds(pl.multiple_of(k * T, T), T), :],
                (((0,), (0,)), ((), ())),
                preferred_element_type=F32,
            )
            return carry

        lax.fori_loop(0, 4, share, 0, unroll=True)

    def ar_send(i, src, dst, device):
        send(src, dst, send_sem.at[4 if i == 0 else 5], ar_r.at[i], device)

    def ar_arrived(i, dst):
        arrived(dst, send_sem.at[4], ar_r.at[i], sibling)

    def z_rows(step):
        return pl.ds(lax.rem(z + step, 8) * 16, 16)

    def relay2(q, zu):
        xc[q, zu] = (x1[q, zu].astype(F32) + e1[q, zu, ahead_of(zu)].astype(F32)).astype(BF16)
        sum_send2(2, q, zu)

    def total2(q, zu):
        return e1[q, zu, 0].astype(F32) + x2[q, zu].astype(F32) + x3[q, zu].astype(F32)

    ar_send(0, w0, a1, sibling)
    fsum_arrived(0, 4)
    fsum_arrived(1, 12)
    for d in order:
        owner = ring(zh, d)
        he[owner] = (h1[owner].astype(F32) + shard(F, owner, core)[...].astype(F32)).astype(BF16)
    ar_arrived(0, a1)
    s1[...] = a1[...] + w0[...]
    for d in range(1, 8):
        ar_send(1, s1.at[z_rows(d)], a2.at[d - 1], on_z(d))
    for kind in (0, 1):
        for h in halves:
            fsum_send(kind, h)
    ar_arrived(1, a2)
    a3[y] = s1[z_rows(0), :] + ((a2[0] + a2[1]) + (a2[2] + a2[3])) + ((a2[4] + a2[5]) + a2[6])
    for d in (1, 2, 3):
        ar_send(2, a3.at[y], a3.at[y], on_y[d])
    total1(2)
    for q, zu in both:
        sum_send2(0, q, zu)
    relay(0)
    fsum_arrived(2, 4)
    for h in halves:
        step = 1 if h == 0 else 3
        uc[h] = (u1[h].astype(F32) + he[ring(zh, step), pl.ds(2 * h, 2)].astype(F32)).astype(BF16)
        fsum_send(2, h)
    total1(1)
    total1(3)
    for q in halves:
        sum_send2(1, q, far)
    ar_arrived(2, a2.at[pl.ds(0, 3)])
    a4[x] = (a3[0] + a3[1]) + (a3[2] + a3[3])
    for d in (1, 2, 3):
        ar_send(3, a4.at[x], a4.at[x], on_x[d])
    sum_arrived(8, 8)
    for q in halves:
        relay2(q, far)
    for q in halves:
        sum_send2(1, q, near)
    for q in halves:
        relay2(q, near)
    total1(0)
    ar_arrived(3, a2.at[pl.ds(0, 3)])
    full[z_rows(0), :] = (a4[0] + a4[1]) + (a4[2] + a4[3])
    for d in range(1, 8):
        ar_send(4, full.at[z_rows(0)], full.at[z_rows(0)], on_z(d))
    sum_arrived(9 + far, 8)
    for q in halves:
        e2[q] = total2(q, far).astype(BF16)
        send(e2.at[q], bz.at[q], send_sem.at[2], sum_r.at[11], partner)

    fsum_arrived(3, 8)
    for n in range(4):
        h, k = n // 2, n % 2
        hidden = he[zh, n].astype(F32) + u2[h, k].astype(F32) + u3[h, k].astype(F32)
        rows = pl.ds(n * T, T)
        lo[rows, :] = jnp.dot(hidden.astype(BF16), we[...], preferred_element_type=F32).astype(BF16)
    outs = [pltpu.make_async_copy(lo, out_ref, out_sem.at[0])]
    outs[0].start()
    ar_arrived(4, a2)
    outs.append(pltpu.make_async_copy(full, gw_ref, out_sem.at[1]))
    outs[1].start()
    sum_arrived(9 + near, 8)
    sum_arrived(11, 4)
    for q in halves:
        mine = total2(q, near) + bz[q].astype(F32)
        for k in (0, 1):
            n = 2 * q + k
            gi[pl.ds(n * T, T), :] = (cscale[n] * jnp.transpose(mine[k])).astype(BF16)
    outs.append(pltpu.make_async_copy(gi, gin_ref, out_sem.at[2]))
    outs[2].start()

    sent(X.at[pl.ds(0, 124)], send_sem.at[0], row_r.at[0], sibling)
    sent(C.at[pl.ds(0, 7)], send_sem.at[1], col_r.at[0], sibling)
    sent(D.at[pl.ds(0, 124)], send_sem.at[2], sum_r.at[0], sibling)
    sent(F.at[pl.ds(0, 28)], send_sem.at[3], fsum_r.at[0], sibling)
    sent(w0, send_sem.at[4], ar_r.at[0], sibling)
    sent(pad, send_sem.at[5], ar_r.at[0], sibling)
    for copy in outs:
        copy.wait()


def leave(*refs):
    n = len(refs) // 2
    for src, dst in zip(refs[:n], refs[n:]):
        dst[...] = src[...]


def body(features, weight, cotangent, tile_values, tile_coords, tile_count, row_degree, col_degree):
    units = lambda *lead: pltpu.VMEM((*lead, 2, T, T), BF16)
    sems = lambda n: pltpu.SemaphoreType.DMA((n,))
    rows = lambda n: pltpu.VMEM((n, T), F32)
    vmem = pl.BlockSpec(memory_space=pltpu.VMEM)
    anywhere = pl.BlockSpec(memory_space=pl.ANY)
    outs = (
        jax.ShapeDtypeStruct((512, T), BF16),
        jax.ShapeDtypeStruct((512, T), BF16),
        jax.ShapeDtypeStruct((T, T), F32),
    )
    results = pl.pallas_call(
        kernel,
        out_shape=outs,
        in_specs=[anywhere] * 8,
        out_specs=(anywhere,) * 3,
        scratch_shapes=[
            pltpu.VMEM((1, 1), jnp.int32),
            pltpu.VMEM((128, T, T), BF16),
            pltpu.VMEM((128, T, T), BF16),
            pltpu.VMEM((8, 528, T), BF16),
            pltpu.VMEM((32, T, T), BF16),
            pltpu.VMEM((128, T, T), BF16),
            pltpu.VMEM((128, T, T), BF16),
            pltpu.VMEM((128, T, T), F32),
            pltpu.VMEM((32, T, T), BF16),
            rows(T),
            pltpu.VMEM((16, T), jnp.int32),
            pltpu.SMEM((16, T), jnp.int32),
            pltpu.VMEM((4, T, T), F32),
            pltpu.VMEM((32, T, T), F32),
            pltpu.VMEM((512, T), BF16),
            pltpu.VMEM((T, T), BF16),
            pltpu.VMEM((2, T), jnp.int32),
            pltpu.VMEM((4, T), jnp.int32),
            pltpu.VMEM((4, T), jnp.int32),
            pltpu.VMEM((512, T), BF16),
            pltpu.VMEM((512, T), BF16),
            units(2, 2, 4), units(2, 2, 4), units(2, 2, 4), units(2, 2, 4), units(2, 2, 4),
            units(2, 2), units(2, 2), units(2, 2), units(2, 2), units(2), units(2),
            pltpu.VMEM((4, 4, T, T), BF16),
            pltpu.VMEM((4, 4, T, T), BF16),
            units(2), units(2), units(2), units(2),
            rows(T),
            rows(T),
            pltpu.VMEM((7, 16, T), F32),
            pltpu.VMEM((4, 16, T), F32),
            pltpu.VMEM((4, 16, T), F32),
            rows(T),
            rows(T),
            rows(320),
            pltpu.SemaphoreType.DMA, sems(7), sems(3), pltpu.SemaphoreType.DMA,
            sems(6), sems(14), sems(12), sems(5), sems(4), sems(6),
        ],
        compiler_params=pltpu.CompilerParams(
            collective_id=0, has_side_effects=True, vmem_limit_bytes=60 * 1024 * 1024
        ),
    )(
        features,
        weight,
        cotangent,
        tile_values[0, 0],
        tile_coords[0, 0].T,
        tile_count,
        row_degree.reshape(4, T),
        col_degree.reshape(4, T),
    )
    return pl.pallas_call(
        leave,
        out_shape=outs,
        in_specs=[vmem] * 3,
        out_specs=(vmem,) * 3,
    )(*results)


def solution(mesh):
    in_specs = (
        P(("col", "row"), None),
        P(),
        P(("row", "col"), None),
        P("row", "col", None, None, None),
        P("row", "col", None, None),
        P("row", "col"),
        P(("row", "col")),
        P(("col", "row")),
    )
    out_specs = (P(("row", "col"), None), P(("col", "row"), None), P())
    return jax.shard_map(body, mesh=mesh, in_specs=in_specs, out_specs=out_specs, check_vma=False)
```

```python
import jax
import jax.numpy as jnp
from jax import lax
from jax.experimental import pallas as pl
from jax.experimental.pallas import tpu as pltpu
from jax.sharding import PartitionSpec as P

MESH = pl.DeviceIdType.MESH
T = 128
F32 = jnp.float32
BF16 = jnp.bfloat16


def ring(place, step):
    return lax.rem(place + step, 4)


def send(src, dst, ssem, rsem, device):
    pltpu.make_async_remote_copy(
        src_ref=src, dst_ref=dst, send_sem=ssem, recv_sem=rsem, device_id=device, device_id_type=MESH
    ).start()


def sent(src, ssem, rsem, device):
    pltpu.make_async_remote_copy(
        src_ref=src, dst_ref=src, send_sem=ssem, recv_sem=rsem, device_id=device, device_id_type=MESH
    ).wait_send()


def arrived(dst, ssem, rsem, device):
    pltpu.make_async_remote_copy(
        src_ref=dst, dst_ref=dst, send_sem=ssem, recv_sem=rsem, device_id=device, device_id_type=MESH
    ).wait_recv()


def kernel(
    feat, weight, cot, values, coords, count, rdeg, cdeg, out_ref, gin_ref, gw_ref,
    cn, X, V, C, G, D, R, Q, F, acc, vtab, stab, cscale, rscale, fe, we, co, rd, cd, lo, gi,
    b1, b2, b3, c1, e1, x1, x2, x3, xc, e2, bz,
    h1, he, u1, u2, u3, uc,
    w0, a1, a2, a3, s1, full, pad,
    load_sem, in_sem, out_sem, tab_sem, send_sem, row_r, sum_r, col_r, fsum_r, ar_r,
):
    r, c = lax.axis_index("row"), lax.axis_index("col")
    zl, y, x = r // 16, lax.rem(r // 4, 4), lax.rem(r, 4)
    zh, core = c // 2, lax.rem(c, 2)
    z = zh * 2 + zl

    px, py = [ring(x, d) for d in range(4)], [ring(y, d) for d in range(4)]
    on_x = [(zl * 16 + y * 4 + px[d], c) for d in range(4)]
    on_y = [(zl * 16 + py[d] * 4 + x, c) for d in range(4)]
    places = ((px, py), (py, px))
    devices = ((on_x, on_y), (on_y, on_x))

    def along(items, step):
        if isinstance(step, int):
            return items[step]
        return jnp.where(step == 1, items[1], items[3])

    def device(q, axis, step):
        there = devices[q][axis]
        if isinstance(step, int):
            return there[step]
        return (jnp.where(step == 1, there[1][0], there[3][0]), c)

    def unit(ref, q, zu, p1, p2):
        i, j = (p1, p2) if q == 0 else (p2, p1)
        return ref.at[pl.ds(64 * zu + 16 * j + 4 * i + 2 * q, 2)]

    def on_zh(step):
        return (r, ring(zh, step) * 2 + core)

    def on_z(step):
        other = lax.rem(z + step, 8)
        return (lax.rem(other, 2) * 16 + y * 4 + x, (other // 2) * 2 + core)

    partner = ((1 - zl) * 16 + y * 4 + x, c)
    sibling = (r, zh * 2 + 1 - core)
    near, far = zl, 1 - zl
    halves = (0, 1)

    ins = [
        pltpu.make_async_copy(src, dst, in_sem.at[i])
        for i, (src, dst) in enumerate(
            ((cdeg, cd), (feat, fe), (rdeg, rd), (cot, C.at[c, pl.ds(0, 512)]), (weight, we), (coords, co), (count, cn))
        )
    ]
    for copy in ins:
        copy.start()
    load = pltpu.make_async_copy(values, V, load_sem)
    load.start()

    barrier = pltpu.get_barrier_semaphore()
    friends = [sibling]
    friends += [on_x[d] for d in (1, 2, 3)]
    friends += [on_y[d] for d in (1, 2, 3)]
    friends += [on_z(d) for d in range(1, 8)]
    friends += [(zl * 16 + py[i] * 4 + px[j], c) for i in (1, 2, 3) for j in (1, 2, 3)]
    for friend in friends:
        pl.semaphore_signal(barrier, inc=1, device_id=friend, device_id_type=MESH)

    def column(line):
        return jnp.transpose(jnp.broadcast_to(1.0 / jnp.sqrt(line.astype(F32)), (T, T)))

    for copy in ins:
        copy.wait()
    for k in range(4):
        cscale[k] = column(cd[k : k + 1, :])
        X[4 * r + k] = (fe[pl.ds(k * T, T), :].astype(F32) * cscale[k]).astype(BF16)
    line = lax.broadcasted_iota(jnp.int32, (16, T), 0)
    tail = jnp.ones((16, T), F32)
    for k in range(4):
        tail = jnp.where(line == k, jnp.broadcast_to(rd[k : k + 1, :].astype(F32), (16, T)), tail)
    C[c, pl.ds(512, 16), :] = tail.astype(BF16)

    pl.semaphore_wait(barrier, len(friends))

    def route(zu, k):
        if k == 0:
            return 0, 1
        if k == 1:
            return 0, 3
        return 3 - 2 * zu, 1 + 2 * zu

    def gather1(q, zu, k):
        first, second = places[q]
        back, ahead = route(zu, k)
        piece = unit(X, q, zu, along(first, back), second[0])
        send(piece, piece, send_sem.at[0], row_r.at[6 * zu + k // 2], device(q, 0, ahead))

    def gather2(q, zu, o, k):
        first, second = places[q]
        back, ahead = route(zu, k)
        piece = unit(X, q, zu, first[o], along(second, back))
        i = 13 if k == 2 else 6 * zu + 2 + o
        send(piece, piece, send_sem.at[0], row_r.at[i], device(q, 1, ahead))

    def gathered(i, tiles):
        arrived(X.at[pl.ds(0, tiles)], send_sem.at[0], row_r.at[i], sibling)

    def shard(ref, zh_of, core_of):
        return ref.at[pl.ds(4 * (zh_of * 2 + core_of), 4)]

    def col_piece(owner_step, i, core_of):
        whose = ring(zh, owner_step) * 2 + core_of
        if i in (2, 7):
            return C.at[whose, pl.ds(0, 256)]
        if i in (3, 8):
            return C.at[whose, pl.ds(256, 272)]
        return C.at[whose]

    def col_send(owner_step, i, device):
        piece = col_piece(owner_step, i, core)
        send(piece, piece, send_sem.at[1], col_r.at[(0, 0, 1, 1, 2, 3, 3, 4, 4)[i]], device)

    def col_arrived(i):
        n = (2, 1, 1, 2, 1)[i]
        arrived(C.at[pl.ds(0, n)], send_sem.at[1], col_r.at[i], sibling)

    def scaled_grad(owner):
        lines = C[owner, pl.ds(512, 16), :].astype(F32)
        for k in range(4):
            n = 4 * owner + k
            scale = column(lines[k : k + 1, :])
            rscale[n] = scale
            grad = lax.dot_general(
                C[owner, pl.ds(k * T, T), :], we[...], (((1,), (1,)), ((), ())), preferred_element_type=F32
            )
            G[n] = jnp.transpose((scale * grad).astype(BF16))

    for q in halves:
        piece = unit(X, q, near, places[q][0][0], places[q][1][0])
        send(piece, piece, send_sem.at[0], row_r.at[12], partner)
    for q in halves:
        gather1(q, near, 0)
        gather1(q, near, 1)
    for q in halves:
        gather2(q, near, 0, 0)
        gather2(q, near, 0, 1)
    col_send(0, 0, on_zh(1))
    col_send(0, 1, on_zh(3))
    col_send(0, 4, sibling)

    own = lax.broadcasted_iota(jnp.int32, (T, T), 0)
    lane = lax.broadcasted_iota(jnp.int32, (T, T), 1)
    live = own < jnp.broadcast_to(cn[...], (T, T))
    by_row = jnp.transpose(jnp.broadcast_to(co[0:1, :], (T, T)))
    by_col = jnp.transpose(jnp.broadcast_to(co[1:2, :], (T, T)))
    def pick(mask, what):
        return jnp.sum(jnp.where(mask, what, 0), axis=0, keepdims=True)

    for base, major, other in ((0, by_col, by_row), (8, by_row, by_col)):
        major = jnp.where(live, major, T)
        key = major * T + own
        rank = pick(key < jnp.transpose(key), jnp.ones_like(key))
        rank = jnp.transpose(jnp.broadcast_to(rank, (T, T)))
        here = rank == lane
        target = pick(here, major)
        before = pick(rank + 1 == lane, major + 1) - 1
        vtab[base : base + 1, :] = pick(here, own)
        vtab[base + 1 : base + 2, :] = pick(here, other)
        vtab[base + 2 : base + 3, :] = (target == before).astype(jnp.int32)
        vtab[base + 3 : base + 4, :] = jnp.maximum(pick(major <= lane, jnp.ones_like(key)) - 1, 0)
        vtab[base + 4 : base + 5, :] = jnp.minimum(pick(major == lane, jnp.ones_like(key)), 1)
    table = pltpu.make_async_copy(vtab, stab, tab_sem)
    table.start()

    def products(base, first, last, source, out, contract):
        def step(i, carry):
            total = acc[...]
            for k in range(8):
                k += 8 * i
                tile = V[stab[base, k]]
                rows = source[stab[base + 1, k]]
                pair = (tile, rows) if contract else (rows, tile)
                prod = jnp.dot(*pair, preferred_element_type=F32)
                total = prod + jnp.where(stab[base + 2, k] == 1, total, 0.0)
                out[k] = total.astype(out.dtype)
            acc[...] = total
            return carry

        lax.fori_loop(first // 8, last // 8, step, 0, unroll=1)

    def segment(base, segments, j):
        return jnp.where(stab[base + 4, j] == 1, segments[stab[base + 3, j]], 0.0)

    def spread(first, last):
        def step(j, carry):
            D[j] = segment(0, R, j).astype(BF16)
            return carry

        lax.fori_loop(first, last, step, 0, unroll=4)

    def turn1(zu):
        gathered(6 * zu, 8)
        for q in halves:
            gather1(q, zu, 2)
        for o in (3, 1):
            for q in halves:
                gather2(q, zu, o, 0)
                gather2(q, zu, o, 1)

    def turn2(zu):
        gathered(6 * zu + 1, 4)
        for q in halves:
            gather2(q, zu, 2, 0)
            gather2(q, zu, 2, 1)

    def turn3(zu, o):
        gathered(6 * zu + 2 + o, 8)
        for q in halves:
            gather2(q, zu, o, 2)

    turn1(near)
    gathered(12, 4)
    for q in halves:
        gather1(q, far, 0)
        gather1(q, far, 1)
    for q in halves:
        gather2(q, far, 0, 0)
        gather2(q, far, 0, 1)
    turn2(near)
    turn3(near, 0)
    scaled_grad(c)
    col_arrived(2)
    scaled_grad(zh * 2 + 1 - core)
    turn1(far)
    turn3(near, 3)
    turn3(near, 1)
    col_arrived(0)
    col_send(3, 2, on_zh(1))
    col_send(1, 3, on_zh(3))
    col_send(3, 5, sibling)
    col_send(1, 6, sibling)
    turn3(far, 0)
    scaled_grad(ring(zh, 3) * 2 + core)
    scaled_grad(ring(zh, 1) * 2 + core)
    turn3(near, 2)
    turn2(far)
    col_arrived(3)
    scaled_grad(ring(zh, 3) * 2 + 1 - core)
    scaled_grad(ring(zh, 1) * 2 + 1 - core)
    col_arrived(1)
    col_send(2, 7, sibling)
    col_send(2, 8, sibling)
    scaled_grad(ring(zh, 2) * 2 + core)
    col_arrived(4)
    scaled_grad(ring(zh, 2) * 2 + 1 - core)
    load.wait()
    table.wait()
    acc[...] = jnp.zeros_like(acc)
    products(0, 0, 24, G, R, 0)
    turn3(far, 3)
    products(0, 24, 48, G, R, 0)
    turn3(far, 1)
    products(0, 48, 128, G, R, 0)
    turn3(far, 2)
    spread(0, 128)

    def ahead_of(zu):
        return 1 + 2 * zu

    def behind_of(zu):
        return 3 - 2 * zu

    def sum_send(kind, q, zu, o):
        first, second = places[q]
        step = behind_of(zu) if kind == 1 else ahead_of(zu)
        if kind == 2:
            src = c1.at[q, zu, o]
        else:
            src = unit(D, q, zu, first[o], second[2] if kind == 0 else along(second, step))
        i = 4 * zu + o if kind == 0 else 8 + 4 * zu + o
        send(src, (b1, b2, b3)[kind].at[q, zu, o], send_sem.at[2], sum_r.at[i], device(q, 1, step))

    def sum_arrived(i, tiles):
        arrived(D.at[pl.ds(0, tiles)], send_sem.at[2], sum_r.at[i], sibling)

    def sum_send2(kind, q, zu):
        step = behind_of(zu) if kind == 1 else ahead_of(zu)
        src = (e1.at[q, zu, 2], e1.at[q, zu, step], xc.at[q, zu])[kind]
        i = 16 + zu if kind == 0 else 18 + zu
        send(src, (x1, x2, x3)[kind].at[q, zu], send_sem.at[2], sum_r.at[i], device(q, 0, step))

    def own_unit(q, zu, o, step):
        first, second = places[q]
        return unit(D, q, zu, first[o], along(second, step))[...].astype(F32)

    order = (2, 1, 3, 0)
    both = [(q, zu) for zu in (far, near) for q in halves]
    for o in order:
        for q, zu in both:
            sum_send(0, q, zu, o)
    for o in order:
        for q in halves:
            sum_send(1, q, far, o)
            sum_send(1, q, near, o)

    gathered(13, 32)

    def relay(zu, o):
        sum_arrived(4 * zu + o, 4)
        for q in halves:
            c1[q, zu, o] = (b1[q, zu, o].astype(F32) + own_unit(q, zu, o, ahead_of(zu))).astype(BF16)
            sum_send(2, q, zu, o)

    def total1(zu, o):
        sum_arrived(8 + 4 * zu + o, 8)
        for q in halves:
            e1[q, zu, o] = (
                own_unit(q, zu, o, 0) + b2[q, zu, o].astype(F32) + b3[q, zu, o].astype(F32)
            ).astype(BF16)

    acc[...] = jnp.zeros_like(acc)
    products(8, 0, 48, X, Q, 1)
    relay(far, 2)
    relay(near, 2)
    products(8, 48, 88, X, Q, 1)
    relay(far, 1)
    relay(near, 1)
    products(8, 88, 128, X, Q, 1)
    relay(far, 3)
    relay(near, 3)

    def scaled(i, carry):
        F[i] = (rscale[i] * segment(8, Q, i)).astype(BF16)
        return carry

    lax.fori_loop(0, 32, scaled, 0, unroll=4)

    def fsum_send(kind, h):
        step = (1 if h == 0 else 3) if kind != 1 else (3 if h == 0 else 1)
        src = (he.at[ring(zh, 2), pl.ds(2 * h, 2)], he.at[ring(zh, step), pl.ds(2 * h, 2)], uc.at[h])[kind]
        send(src, (u1, u2, u3)[kind].at[h], send_sem.at[3], fsum_r.at[2 if kind == 0 else 3], on_zh(step))

    def fsum_arrived(i, tiles):
        arrived(F.at[pl.ds(0, tiles)], send_sem.at[3], fsum_r.at[i], sibling)

    for d in order:
        owner = ring(zh, d)
        send(shard(F, owner, 1 - core), h1.at[owner], send_sem.at[3], fsum_r.at[0 if d == 2 else 1], sibling)

    w0[...] = jnp.zeros_like(w0)
    for owner in range(8):
        w0[...] += lax.dot_general(
            F[pl.ds(4 * owner, 4)].reshape(512, T),
            C[owner, pl.ds(0, 512), :],
            (((0,), (0,)), ((), ())),
            preferred_element_type=F32,
        )

    def ar_send(i, src, dst, device):
        send(src, dst, send_sem.at[4 if i == 0 else 5], ar_r.at[i], device)

    def ar_arrived(i, dst):
        arrived(dst, send_sem.at[4], ar_r.at[i], sibling)

    def z_rows(step):
        return pl.ds(lax.rem(z + step, 8) * 16, 16)

    def relay2(q, zu):
        xc[q, zu] = (x1[q, zu].astype(F32) + e1[q, zu, ahead_of(zu)].astype(F32)).astype(BF16)
        sum_send2(2, q, zu)

    def total2(q, zu):
        return e1[q, zu, 0].astype(F32) + x2[q, zu].astype(F32) + x3[q, zu].astype(F32)

    ar_send(0, w0, a1, sibling)
    fsum_arrived(0, 4)
    fsum_arrived(1, 12)
    for d in order:
        owner = ring(zh, d)
        he[owner] = (h1[owner].astype(F32) + shard(F, owner, core)[...].astype(F32)).astype(BF16)
    ar_arrived(0, a1)
    s1[...] = a1[...] + w0[...]
    for d in range(1, 8):
        ar_send(1, s1.at[z_rows(d)], a2.at[d - 1], on_z(d))
    for kind in (0, 1):
        for h in halves:
            fsum_send(kind, h)
    total1(far, 2)
    for q in halves:
        sum_send2(0, q, far)
    relay(far, 0)
    ar_arrived(1, a2)
    a3[4 * y + x] = s1[z_rows(0), :] + ((a2[0] + a2[1]) + (a2[2] + a2[3])) + ((a2[4] + a2[5]) + a2[6])
    for i in range(4):
        for j in range(4):
            if i or j:
                ar_send(2, a3.at[4 * y + x], a3.at[4 * y + x], (zl * 16 + py[i] * 4 + px[j], c))
    total1(far, 1)
    total1(far, 3)
    for q in halves:
        sum_send2(1, q, far)
    total1(near, 2)
    for q in halves:
        sum_send2(0, q, near)
    relay(near, 0)
    fsum_arrived(2, 4)
    for h in halves:
        step = 1 if h == 0 else 3
        uc[h] = (u1[h].astype(F32) + he[ring(zh, step), pl.ds(2 * h, 2)].astype(F32)).astype(BF16)
        fsum_send(2, h)
    sum_arrived(16 + far, 4)
    for q in halves:
        relay2(q, far)
    ar_arrived(2, a3.at[pl.ds(0, 15)])
    sums = [a3[i] for i in range(16)]
    while len(sums) > 1:
        sums = [sums[i] + sums[i + 1] for i in range(0, len(sums), 2)]
    full[z_rows(0), :] = sums[0]
    for d in range(1, 8):
        ar_send(4, full.at[z_rows(0)], full.at[z_rows(0)], on_z(d))
    total1(near, 1)
    total1(near, 3)
    for q in halves:
        sum_send2(1, q, near)
    sum_arrived(16 + near, 4)
    for q in halves:
        relay2(q, near)
    total1(far, 0)
    sum_arrived(18 + far, 8)
    for q in halves:
        e2[q] = total2(q, far).astype(BF16)
        send(e2.at[q], bz.at[q], send_sem.at[2], sum_r.at[20], partner)
    total1(near, 0)

    fsum_arrived(3, 8)
    for n in range(4):
        h, k = n // 2, n % 2
        hidden = he[zh, n].astype(F32) + u2[h, k].astype(F32) + u3[h, k].astype(F32)
        rows = pl.ds(n * T, T)
        lo[rows, :] = jnp.dot(hidden.astype(BF16), we[...], preferred_element_type=F32).astype(BF16)
    outs = [pltpu.make_async_copy(lo, out_ref, out_sem.at[0])]
    outs[0].start()
    ar_arrived(4, a2)
    outs.append(pltpu.make_async_copy(full, gw_ref, out_sem.at[1]))
    outs[1].start()
    sum_arrived(18 + near, 8)
    sum_arrived(20, 4)
    for q in halves:
        mine = total2(q, near) + bz[q].astype(F32)
        for k in (0, 1):
            n = 2 * q + k
            gi[pl.ds(n * T, T), :] = (cscale[n] * jnp.transpose(mine[k])).astype(BF16)
    outs.append(pltpu.make_async_copy(gi, gin_ref, out_sem.at[2]))
    outs[2].start()

    sent(X.at[pl.ds(0, 124)], send_sem.at[0], row_r.at[0], sibling)
    sent(C.at[pl.ds(0, 7)], send_sem.at[1], col_r.at[0], sibling)
    sent(D.at[pl.ds(0, 124)], send_sem.at[2], sum_r.at[0], sibling)
    sent(F.at[pl.ds(0, 28)], send_sem.at[3], fsum_r.at[0], sibling)
    sent(w0, send_sem.at[4], ar_r.at[0], sibling)
    sent(pad, send_sem.at[5], ar_r.at[0], sibling)
    for copy in outs:
        copy.wait()


def leave(*refs):
    sources, results, held, arrive, depart = refs[:3], refs[3:6], refs[6:9], refs[9], refs[10]
    first = [pltpu.make_async_copy(sources[i], held[i], arrive.at[i]) for i in range(3)]
    second = [pltpu.make_async_copy(held[i], results[i], depart.at[i]) for i in range(3)]
    for copy in first:
        copy.start()
    for here, there in zip(first, second):
        here.wait()
        there.start()
    for copy in second:
        copy.wait()


def body(features, weight, cotangent, tile_values, tile_coords, tile_count, row_degree, col_degree):
    units = lambda *lead: pltpu.VMEM((*lead, 2, T, T), BF16)
    sems = lambda n: pltpu.SemaphoreType.DMA((n,))
    rows = lambda n: pltpu.VMEM((n, T), F32)
    anywhere = pl.BlockSpec(memory_space=pl.ANY)
    outs = (
        jax.ShapeDtypeStruct((512, T), BF16),
        jax.ShapeDtypeStruct((512, T), BF16),
        jax.ShapeDtypeStruct((T, T), F32),
    )
    results = pl.pallas_call(
        kernel,
        out_shape=outs,
        in_specs=[anywhere] * 8,
        out_specs=(anywhere,) * 3,
        scratch_shapes=[
            pltpu.VMEM((1, 1), jnp.int32),
            pltpu.VMEM((128, T, T), BF16),
            pltpu.VMEM((128, T, T), BF16),
            pltpu.VMEM((8, 528, T), BF16),
            pltpu.VMEM((32, T, T), BF16),
            pltpu.VMEM((128, T, T), BF16),
            pltpu.VMEM((128, T, T), BF16),
            pltpu.VMEM((128, T, T), F32),
            pltpu.VMEM((32, T, T), BF16),
            rows(T),
            pltpu.VMEM((16, T), jnp.int32),
            pltpu.SMEM((16, T), jnp.int32),
            pltpu.VMEM((4, T, T), F32),
            pltpu.VMEM((32, T, T), F32),
            pltpu.VMEM((512, T), BF16),
            pltpu.VMEM((T, T), BF16),
            pltpu.VMEM((2, T), jnp.int32),
            pltpu.VMEM((4, T), jnp.int32),
            pltpu.VMEM((4, T), jnp.int32),
            pltpu.VMEM((512, T), BF16),
            pltpu.VMEM((512, T), BF16),
            units(2, 2, 4), units(2, 2, 4), units(2, 2, 4), units(2, 2, 4), units(2, 2, 4),
            units(2, 2), units(2, 2), units(2, 2), units(2, 2), units(2), units(2),
            pltpu.VMEM((4, 4, T, T), BF16),
            pltpu.VMEM((4, 4, T, T), BF16),
            units(2), units(2), units(2), units(2),
            rows(T),
            rows(T),
            pltpu.VMEM((7, 16, T), F32),
            pltpu.VMEM((16, 16, T), F32),
            rows(T),
            rows(T),
            rows(464),
            pltpu.SemaphoreType.DMA, sems(7), sems(3), pltpu.SemaphoreType.DMA,
            sems(6), sems(14), sems(21), sems(5), sems(4), sems(6),
        ],
        compiler_params=pltpu.CompilerParams(
            collective_id=0, has_side_effects=True, vmem_limit_bytes=60 * 1024 * 1024
        ),
    )(
        features,
        weight,
        cotangent,
        tile_values[0, 0],
        tile_coords[0, 0].T,
        tile_count,
        row_degree.reshape(4, T),
        col_degree.reshape(4, T),
    )
    return pl.pallas_call(
        leave,
        out_shape=outs,
        in_specs=[anywhere] * 3,
        out_specs=(anywhere,) * 3,
        scratch_shapes=[*(pltpu.VMEM(out.shape, out.dtype) for out in outs), sems(3), sems(3)],
    )(*results)


def solution(mesh):
    in_specs = (
        P(("col", "row"), None),
        P(),
        P(("row", "col"), None),
        P("row", "col", None, None, None),
        P("row", "col", None, None),
        P("row", "col"),
        P(("row", "col")),
        P(("col", "row")),
    )
    out_specs = (P(("row", "col"), None), P(("col", "row"), None), P())
    return jax.shard_map(body, mesh=mesh, in_specs=in_specs, out_specs=out_specs, check_vma=False)
```
